32 devices in a mesh: gx: 16 (over z, y, core), gy: 2 (over x).
Axes of the slice: x: 2, y: 2, z: 4, core: 2. Of those that a mesh axis runs over, the one named last changes fastest.
Arguments:
- latents: bfloat16 [16, 2, 1024, 128], P('gx', 'gy'), may hold values from -6 to 6
- mig_rows: int32 [16, 2, 4, 64], P('gx', 'gy'), may hold values from 0 to 1023, as said below
- mig_count: int32 [16, 2, 4], P('gx', 'gy'), may hold values from 0 to 64, as said below
- ghost_rows: int32 [16, 2, 8, 256], P('gx', 'gy'), may hold values from 0 to 1279, as said below
- ghost_count: int32 [16, 2, 8], P('gx', 'gy'), may hold values from 0 to 256, as said below
- neighbours: int32 [16, 2, 16, 80], P('gx', 'gy'), may hold values from -1 to 3327, as said below
- geometry: float32 [16, 2, 4, 16, 1280], P('gx', 'gy'), may hold values from -1 to 1
- edge_w: bfloat16 [2, 3, 128, 128], replicated, may hold values from -0.5 to 0.5
- node_w: bfloat16 [2, 3, 128, 128], replicated, may hold values from -0.5 to 0.5
- geo_w: float32 [2, 4, 128], replicated, may hold values from -3 to 3
- biases: float32 [2, 4, 128], replicated, may hold values from -3 to 3
- gains: float32 [2, 2, 128], replicated, may hold values from 0.1 to 1.9
Outputs:
- updated: bfloat16 [16, 2, 1280, 128], P('gx', 'gy')
The draws below stay inside these ranges and needn't reach their ends.
Inputs may be any that keep to these rules, and one draw needn't show every extreme that they name: `mig_rows`: within one device all 256 entries are distinct rows. `mig_count`: zero towards the outside of the device grid; some device sends 64 rows in some direction. `ghost_rows`: rows of the device's block after migration. `ghost_count`: zero towards the outside of the device grid; some device fills all 256 slots towards some neighbour. `neighbours`: -1 marks an empty slot; other values are rows of the device's table. A slot of a tile is shared by the tile's 16 rows.
All inputs are finite; a program needn't handle non-finite values.
Results may differ from the reference program's by a relative error of at most 0.0061.
Values may be sent and summed in bfloat16 or wider, within the bound.
No kernel may reach another device: no remote copies, remote signals or barrier semaphores. Data moves between devices by JAX's collectives and lax.ppermute only.
A program may use at most 64 MiB of HBM per device.

```python
import jax
import jax.numpy as jnp
from jax import lax

LATENT = 128
NEIGH = 16
LAYERS = 2
PART_DEV = 1024
MIG = 64
GHOST = 256
ROWS = 1280
TILES = 80
TABLE = 3328
N_GX = 16
N_GY = 2


OFFSETS = ((-1, -1), (-1, 0), (-1, 1), (0, -1), (0, 1), (1, -1), (1, 0), (1, 1))


MOVES = ((-1, 0), (1, 0), (0, -1), (0, 1))


def inside_grid(step_x, step_y):
    place_x = jnp.arange(N_GX)[:, None] + step_x
    place_y = jnp.arange(N_GY)[None, :] + step_y
    return (place_x >= 0) & (place_x < N_GX) & (place_y >= 0) & (place_y < N_GY)


def draw_mig_rows(key, part):
    key = jax.random.fold_in(key, 11)
    subkeys = jax.random.split(key, N_GX * N_GY)
    chosen = jax.vmap(lambda subkey: jax.random.permutation(subkey, PART_DEV)[:4 * MIG])(subkeys)
    return chosen.reshape(N_GX, N_GY, 4, MIG).astype(jnp.int32)


def draw_mig_count(key, part):
    key = jax.random.fold_in(key, 12)
    counts = jnp.minimum(jax.random.randint(key, (N_GX, N_GY, 4), 0, 2 * MIG + 1), MIG)
    reachable = jnp.stack([inside_grid(step_x, step_y) for step_x, step_y in MOVES], axis=-1)
    counts = jnp.where(reachable, counts, 0)
    return counts.at[0, 0, 1].set(MIG).astype(jnp.int32)


def draw_ghost_rows(key, part):
    key = jax.random.fold_in(key, 13)
    return jax.random.randint(key, (N_GX, N_GY, 8, GHOST), 0, ROWS).astype(jnp.int32)


def draw_ghost_count(key, part):
    key = jax.random.fold_in(key, 14)
    counts = jnp.minimum(jax.random.randint(key, (N_GX, N_GY, 8), 0, 2 * GHOST + 1), GHOST)
    reachable = jnp.stack([inside_grid(step_x, step_y) for step_x, step_y in OFFSETS], axis=-1)
    counts = jnp.where(reachable, counts, 0)
    return counts.at[0, 0, 6].set(GHOST).astype(jnp.int32)


def draw_neighbours(key, part):
    key = jax.random.fold_in(key, 15)
    kind_key, local_key, ghost_key = jax.random.split(key, 3)
    shape = (N_GX, N_GY, NEIGH, TILES)
    kinds = jax.random.randint(kind_key, shape, 0, 16)
    local_rows = jax.random.randint(local_key, shape, 0, ROWS)
    ghost_slots = jax.random.randint(ghost_key, shape, ROWS, TABLE)
    picked = jnp.where(kinds < 3, -1, jnp.where(kinds < 9, local_rows, ghost_slots))
    picked = picked.at[0, 0, 0, 0].set(TABLE - 1)
    return picked.astype(jnp.int32)


def levels(key, extent, cuts, smallest, top_value):
    loudness, own = 1.0, jax.random.fold_in(key, 6)
    for axis_at, parts in cuts:
        heights = jnp.exp(jax.random.uniform(jax.random.fold_in(own, axis_at), (parts,), jnp.float32, smallest / len(cuts), top_value / len(cuts)))
        loudness = loudness * jnp.repeat(heights, extent[axis_at] // parts).reshape([-1 if axis == axis_at else 1 for axis in range(len(extent))])
    return loudness


def normal_values(key, dims, scale, bound, pieces=(), held_as=jnp.bfloat16):
    drawn = jax.random.normal(key, dims, jnp.float32) * scale
    if len(pieces) > 0:
        drawn = levels(key, dims, pieces, -0.22, 0.18) * drawn
    return jnp.clip(drawn, min=-bound, max=bound).astype(held_as)


def setup_inputs(seed: int = 0) -> dict:
    key_of = jax.random.split(jax.random.key(seed), 13)
    latents = normal_values(key_of[0], (N_GX, N_GY, PART_DEV, LATENT), 1.0, 6.0, ((0, 16), (1, 2)))
    mig_rows = draw_mig_rows(jax.random.fold_in(key_of[12], 71), 0)
    mig_count = draw_mig_count(jax.random.fold_in(key_of[12], 71), 0)
    ghost_rows = draw_ghost_rows(jax.random.fold_in(key_of[12], 71), 0)
    ghost_count = draw_ghost_count(jax.random.fold_in(key_of[12], 71), 0)
    neighbours = draw_neighbours(jax.random.fold_in(key_of[12], 71), 0)
    geometry = jnp.clip(jax.random.uniform(key_of[6], (N_GX, N_GY, 4, NEIGH, ROWS), jnp.float32, -1.0, 1.0) * levels(key_of[6], (N_GX, N_GY, 4, NEIGH, ROWS), ((0, 16), (1, 2)), -0.4, 0.0), -1.0, 1.0)
    edge_w = normal_values(key_of[7], (LAYERS, 3, LATENT, LATENT), LATENT ** -0.5, 0.5)
    node_w = normal_values(key_of[8], (LAYERS, 3, LATENT, LATENT), LATENT ** -0.5, 0.5)
    geo_w = normal_values(key_of[9], (LAYERS, 4, LATENT), 4 ** -0.5, 3.0, (), jnp.float32)
    biases = normal_values(key_of[10], (LAYERS, 4, LATENT), 0.5, 3.0, (), jnp.float32)
    gains = jnp.clip(1.0 + 0.18 * jax.random.normal(key_of[11], (LAYERS, 2, LATENT), jnp.float32), 0.1, 1.9)
    return {"latents": latents, "mig_rows": mig_rows, "mig_count": mig_count, "ghost_rows": ghost_rows, "ghost_count": ghost_count, "neighbours": neighbours, "geometry": geometry, "edge_w": edge_w, "node_w": node_w, "geo_w": geo_w, "biases": biases, "gains": gains}


OFFSETS = ((-1, -1), (-1, 0), (-1, 1), (0, -1), (0, 1), (1, -1), (1, 0), (1, 1))

def layer_norm(values, gain):
    center = values - lax.optimization_barrier(jnp.mean(values, axis=-1, keepdims=True))
    spread = lax.optimization_barrier(jnp.mean(center * center, axis=-1, keepdims=True))
    return center * lax.rsqrt(spread + 1e-05) * gain

def shift_grid(array, axis, offset):
    if offset == 0:
        return array
    length = array.shape[axis]
    zero_part = jnp.zeros_like(lax.slice_in_dim(array, 0, 1, axis=axis))
    if offset > 0:
        return jnp.concatenate([zero_part, lax.slice_in_dim(array, 0, length - 1, axis=axis)], axis=axis)
    return jnp.concatenate([lax.slice_in_dim(array, 1, length, axis=axis), zero_part], axis=axis)

def pick_rows(array, rows):
    return jax.vmap(jax.vmap(lambda block, where_rows: block[where_rows]))(array, rows)

def device_layer(table, tile_links, edge_feats, edge_mats, node_mats, geo_rows, bias_rows, gain_rows):
    tile_size = tile_links.shape[0]
    row_total = tile_links.shape[1] * tile_size
    live_tile = tile_links >= 0
    sender_row = jnp.where(live_tile, tile_links, 0)
    live_edge = jnp.repeat(live_tile, tile_size, axis=1)
    table_wide = table.astype(jnp.float32)
    extended = table_wide[:row_total]
    sender_part = jnp.dot(table_wide, edge_mats[1].astype(jnp.float32))
    receiver_part = jnp.dot(extended, edge_mats[0].astype(jnp.float32))
    geo_term = edge_feats[0][..., None] * geo_rows[0]
    for channel in range(1, 4):
        geo_term = geo_term + edge_feats[channel][..., None] * geo_rows[channel]
    sender_edges = jnp.repeat(sender_part[sender_row], tile_size, axis=1)
    first_sum = sender_edges + receiver_part[None] + geo_term + bias_rows[0]
    hidden = jnp.maximum(first_sum, 0.0).astype(jnp.bfloat16)
    width = hidden.shape[-1]
    second = jnp.dot(hidden.reshape(-1, width).astype(jnp.float32), edge_mats[2].astype(jnp.float32))
    second = second.reshape(hidden.shape) + bias_rows[1]
    message = layer_norm(second, gain_rows[0])
    gathered = lax.optimization_barrier(jnp.sum(jnp.where(live_edge[..., None], message, 0.0), axis=0)).astype(jnp.bfloat16)
    node_first = jnp.dot(extended, node_mats[0].astype(jnp.float32))
    node_first = node_first + jnp.dot(gathered.astype(jnp.float32), node_mats[1].astype(jnp.float32)) + bias_rows[2]
    node_hidden = jnp.maximum(node_first, 0.0).astype(jnp.bfloat16)
    node_out = jnp.dot(node_hidden.astype(jnp.float32), node_mats[2].astype(jnp.float32)) + bias_rows[3]
    return (extended + layer_norm(node_out, gain_rows[1])).astype(jnp.bfloat16)

def reference(latents, mig_rows, mig_count, ghost_rows, ghost_count, neighbours, geometry, edge_w, node_w, geo_w, biases, gains):
    grid_x, grid_y = (latents.shape[0], latents.shape[1])
    zero_value = jnp.zeros((), jnp.bfloat16)
    valid_leave = jnp.arange(MIG)[None, None, None, :] < mig_count[..., None]
    flat_rows = mig_rows.reshape(grid_x, grid_y, 4 * MIG)
    picked = pick_rows(latents, flat_rows).reshape(grid_x, grid_y, 4, MIG, LATENT)
    packets = jnp.where(valid_leave[..., None], picked, zero_value)
    marks = jax.vmap(lambda leave_list, leave_flag: jnp.zeros((PART_DEV,), jnp.int32).at[leave_list].max(leave_flag))(flat_rows.reshape(-1, 4 * MIG), valid_leave.reshape(-1, 4 * MIG).astype(jnp.int32))
    retained = jnp.where(marks.reshape(grid_x, grid_y, PART_DEV)[..., None] > 0, zero_value, latents)
    arrivals = [shift_grid(packets[:, :, 1], 0, 1), shift_grid(packets[:, :, 0], 0, -1), shift_grid(packets[:, :, 3], 1, 1), shift_grid(packets[:, :, 2], 1, -1)]
    extended = jnp.concatenate([retained] + arrivals, axis=2)
    ghost_ok = jnp.arange(GHOST)[None, None, None, :] < ghost_count[..., None]
    flat_ghost = ghost_rows.reshape(grid_x, grid_y, 8 * GHOST)
    flat_links = neighbours.reshape(-1, NEIGH, TILES)
    flat_feats = geometry.reshape(-1, 4, NEIGH, ROWS)
    for layer in range(LAYERS):
        chosen = pick_rows(extended, flat_ghost).reshape(grid_x, grid_y, 8, GHOST, LATENT)
        outgoing = jnp.where(ghost_ok[..., None], chosen, zero_value)
        landed = [shift_grid(shift_grid(outgoing[:, :, position], 0, step_x), 1, step_y) for position, (step_x, step_y) in enumerate(OFFSETS)]
        table = jnp.concatenate([extended] + landed, axis=2).reshape(-1, TABLE, LATENT)

        def one_device(inputs, layer=layer):
            return device_layer(inputs[0], inputs[1], inputs[2], edge_w[layer], node_w[layer], geo_w[layer], biases[layer], gains[layer])
        extended = lax.map(one_device, (table, flat_links, flat_feats)).reshape(grid_x, grid_y, ROWS, LATENT)
    return extended
```

```python
import functools
import itertools
import math

import jax
import jax.numpy as jnp
from jax import lax
from jax.experimental import pallas as pl
from jax.experimental.pallas import tpu as pltpu
from jax.sharding import PartitionSpec as P

F32 = jnp.float32
BF16 = jnp.bfloat16
CHUNK = 128
VMEM = pl.BlockSpec(memory_space=pltpu.VMEM)
SMEM = pl.BlockSpec(memory_space=pltpu.SMEM)
PARAMS = pltpu.CompilerParams(vmem_limit_bytes=48 * 1024 * 1024)


def partner(place, count, kind):
    other = place + 1 if place % 2 == kind else place - 1
    return other if 0 <= other < count else None


def kinds(count):
    return [0, 1][: max(0, min(2, count - 1))]


def links(count_x, count_y):
    both = itertools.product([None] + kinds(count_x), [None] + kinds(count_y))
    return [pair for pair in both if pair != (None, None)]


def swap(value, link):
    count_x, count_y = lax.axis_size("gx"), lax.axis_size("gy")
    pairs = []
    for x, y in itertools.product(range(count_x), range(count_y)):
        to_x = x if link[0] is None else partner(x, count_x, link[0])
        to_y = y if link[1] is None else partner(y, count_y, link[1])
        if to_x is not None and to_y is not None:
            pairs.append((x * count_y + y, to_x * count_y + to_y))
    return lax.ppermute(value, ("gx", "gy"), pairs)


def step(axis, kind):
    if kind is None:
        return 0
    sign = 1 if kind == 0 else -1
    return sign * (1 - 2 * lax.rem(lax.axis_index(axis), 2))


def section(step_x, step_y):
    place = (step_x + 1) * 3 + step_y + 1
    return jnp.where(place > 4, place - 1, place)


def side(link):
    if link[1] is None:
        return (step("gx", link[0]) + 1) // 2
    return 2 + (step("gy", link[1]) + 1) // 2


def pack_kernel(sides, latents_ref, rows_ref, count_ref, retained_ref, *packet_refs):
    total = latents_ref.shape[0]
    slots = rows_ref.shape[1]
    owned = latents_ref[...]
    row_id = lax.broadcasted_iota(jnp.int32, (total, slots), 0)
    lane = lax.broadcasted_iota(jnp.int32, (1, slots), 1)

    def picker(direction):
        wanted = rows_ref[pl.ds(direction, 1), :]
        wanted = jnp.where(lane < count_ref[direction], wanted, -1)
        return (row_id == wanted).astype(F32)

    marks = picker(0)
    for direction in range(1, 4):
        marks = marks + picker(direction)
    marks = jnp.dot(marks.astype(BF16), jnp.ones((slots, owned.shape[1]), BF16), preferred_element_type=F32)
    retained_ref[...] = jnp.where(marks > 0.0, 0.0, owned.astype(F32)).astype(BF16)
    for link, packet_ref in zip(sides, packet_refs):
        chosen = lax.dot_general(
            picker(side(link)).astype(BF16), owned, (((0,), (0,)), ((), ())), preferred_element_type=F32
        )
        packet_ref[...] = chosen.astype(BF16)


def gather_ghosts(all_links, extended_ref, rows_ref, count_ref, send_refs):
    total, width = extended_ref.shape
    slots = rows_ref.shape[1]
    lane = lax.broadcasted_iota(jnp.int32, (1, slots), 1)
    column = lax.broadcasted_iota(jnp.int32, (slots, 128), 1).astype(F32)
    for link, send_ref in zip(all_links, send_refs):
        target = section(step("gx", link[0]), step("gy", link[1]))
        wanted = rows_ref[pl.ds(target, 1), :]
        wanted = jnp.where(lane < count_ref[target], wanted, -1).astype(F32)
        wanted = jnp.transpose(jnp.broadcast_to(wanted, (128, slots)))
        picker = jnp.concatenate(
            [jnp.where(wanted == column + float(start), 1.0, 0.0).astype(BF16) for start in range(0, total, 128)],
            axis=1,
        )
        send_ref[...] = jnp.dot(picker, extended_ref[...], preferred_element_type=F32).astype(BF16)


def build_kernel(sides, all_links, retained_ref, *refs):
    arrivals, refs = refs[: len(sides)], refs[len(sides) :]
    rows_ref, count_ref, extended_ref, *send_refs = refs
    total = extended_ref.shape[0]
    owned = retained_ref.shape[0]
    slots = (total - owned) // 4
    extended_ref[pl.ds(0, owned), :] = retained_ref[...]
    extended_ref[pl.ds(owned, total - owned), :] = jnp.zeros((total - owned, extended_ref.shape[1]), BF16)
    for link, arrival_ref in zip(sides, arrivals):
        start = pl.multiple_of(owned + slots * side(link), 16)
        extended_ref[pl.ds(start, slots), :] = arrival_ref[...]
    gather_ghosts(all_links, extended_ref, rows_ref, count_ref, send_refs)


def turn_kernel(geometry_ref, turned_ref):
    feats = geometry_ref[...]
    high = feats.astype(BF16).astype(F32)
    turned_ref[...] = jnp.transpose(jnp.concatenate([high, feats - high], axis=0)).astype(BF16)


def spread_of(center):
    return jnp.sum(center * center, axis=-1, keepdims=True)


def layer_kernel(
    layer, last, all_links, extended_ref, turned_ref, links_ref, edge_ref, node_ref, geo_ref, bias_ref, gain_ref, *refs
):
    landed, refs = refs[: len(all_links)], refs[len(all_links) :]
    if not last:
        rows_ref, count_ref, *refs = refs
    updated_ref, refs = refs[0], refs[1:]
    send_refs, refs = (() if last else refs[: len(all_links)]), (refs if last else refs[len(all_links) :])
    table_ref, first_ref, second_ref, total_ref = refs
    rows_total, width = extended_ref.shape
    slots, tiles = links_ref.shape
    rows = rows_total // tiles
    ghosts = landed[0].shape[0]
    turned_width = turned_ref.shape[1]

    bias_first = bias_ref[layer, pl.ds(0, 1), :]
    sender_mat = edge_ref[layer, 1]
    table_ref[pl.ds(0, rows_total), :] = (
        jnp.dot(extended_ref[...], sender_mat, preferred_element_type=F32) + bias_first
    )
    if len(all_links) < 8:
        table_ref[pl.ds(rows_total, 8 * ghosts), :] = jnp.broadcast_to(bias_first, (8 * ghosts, width))
    for link, landed_ref in zip(all_links, landed):
        source = section(-step("gx", link[0]), -step("gy", link[1]))
        start = pl.multiple_of(rows_total + ghosts * source, 16)
        table_ref[pl.ds(start, ghosts), :] = (
            jnp.dot(landed_ref[...], sender_mat, preferred_element_type=F32) + bias_first
        )

    channels = geo_ref.shape[1]
    spread_geo = jnp.concatenate(
        [jnp.broadcast_to(geo_ref[layer, pl.ds(c, 1), :], (slots, width)) for c in range(channels)], axis=0
    )
    slot_of = lax.rem(lax.broadcasted_iota(jnp.int32, (channels * slots, width), 0), slots)
    for slot in range(slots):
        part = jnp.where(slot_of == slot, spread_geo, 0.0).astype(BF16)
        first_ref[pl.ds(0, channels * slots), pl.ds(slot * width, width)] = part
        first_ref[pl.ds(channels * slots, channels * slots), pl.ds(slot * width, width)] = part
        first_ref[pl.ds(turned_width, width), pl.ds(slot * width, width)] = edge_ref[layer, 0]
    edge_second = edge_ref[layer, 2].astype(F32)
    edge_second = (edge_second - jnp.mean(edge_second, axis=-1, keepdims=True)).astype(BF16)
    second_ref[...] = jnp.zeros(second_ref.shape, BF16)
    second_ref[pl.ds(0, width), pl.ds(0, width)] = edge_second
    second_ref[pl.ds(width, width), pl.ds(width, width)] = edge_second
    bias_second = bias_ref[layer, pl.ds(1, 1), :]
    bias_second = bias_second - jnp.mean(bias_second, axis=-1, keepdims=True)

    chunk_tiles = CHUNK // rows

    @pl.loop(0, rows_total // CHUNK)
    def _(chunk):
        start = pl.multiple_of(chunk * CHUNK, CHUNK)
        own = jnp.concatenate([turned_ref[pl.ds(start, CHUNK), :], extended_ref[pl.ds(start, CHUNK), :]], axis=1)
        sums = [jnp.zeros((rows, width), F32) for _ in range(chunk_tiles)]
        for pair in range(0, slots, 2):
            first = jnp.dot(own, first_ref[:, pl.ds(pair * width, 2 * width)], preferred_element_type=F32)
            halves, limits = [], []
            for slot in (pair, pair + 1):
                senders = []
                for tile in range(chunk_tiles):
                    row = links_ref[slot, chunk * chunk_tiles + tile]
                    limits.append(jnp.where(row >= 0, width * 1e-5, jnp.inf))
                    picked = table_ref[pl.ds(jnp.maximum(row, 0), 1), :]
                    senders.append(jnp.broadcast_to(picked, (rows, width)))
                halves.append(jnp.concatenate(senders, axis=0))
            hidden = jnp.maximum(first + jnp.concatenate(halves, axis=1), 0.0).astype(BF16)
            second = jnp.dot(hidden, second_ref[...], preferred_element_type=F32)
            for half in range(2):
                for tile in range(chunk_tiles):
                    center = second[tile * rows : (tile + 1) * rows, half * width : (half + 1) * width] + bias_second
                    scale = lax.rsqrt(spread_of(center) + limits[half * chunk_tiles + tile])
                    sums[tile] = sums[tile] + center * scale
        total_ref[pl.ds(start, CHUNK), :] = jnp.concatenate(sums, axis=0)

    gathered = (total_ref[...] * (gain_ref[layer, pl.ds(0, 1), :] * math.sqrt(width))).astype(BF16)
    extended = extended_ref[...]
    node_first = jnp.dot(
        jnp.concatenate([extended, gathered], axis=1),
        jnp.concatenate([node_ref[layer, 0], node_ref[layer, 1]], axis=0),
        preferred_element_type=F32,
    )
    node_hidden = jnp.maximum(node_first + bias_ref[layer, pl.ds(2, 1), :], 0.0).astype(BF16)
    node_out = jnp.dot(node_hidden, node_ref[layer, 2], preferred_element_type=F32) + bias_ref[layer, pl.ds(3, 1), :]
    center = node_out - jnp.mean(node_out, axis=-1, keepdims=True)
    scale = lax.rsqrt(spread_of(center) / width + 1e-5)
    updated_ref[...] = (extended.astype(F32) + center * scale * gain_ref[layer, pl.ds(1, 1), :]).astype(BF16)
    if not last:
        gather_ghosts(all_links, updated_ref, rows_ref, count_ref, send_refs)


def body(
    latents, mig_rows, mig_count, ghost_rows, ghost_count, neighbours, geometry, edge_w, node_w, geo_w, biases, gains
):
    owned = latents[0, 0]
    leave_rows, leave_count = mig_rows[0, 0], mig_count[0, 0]
    ghost_list, ghost_total = ghost_rows[0, 0], ghost_count[0, 0]
    tile_links = neighbours[0, 0]
    width = owned.shape[1]
    slots, tiles = tile_links.shape
    rows_total = geometry.shape[-1]
    ghosts = ghost_list.shape[1]
    table_rows = rows_total + 8 * ghosts
    all_links = links(lax.axis_size("gx"), lax.axis_size("gy"))
    sides = [link for link in all_links if None in link]
    rows_of = lambda count: jax.ShapeDtypeStruct((count, width), BF16)

    retained, *packets = pl.pallas_call(
        functools.partial(pack_kernel, sides),
        out_shape=[rows_of(owned.shape[0])] + [rows_of(leave_rows.shape[1])] * len(sides),
        in_specs=[VMEM, VMEM, SMEM],
        out_specs=[VMEM] * (1 + len(sides)),
        compiler_params=PARAMS,
        name="pack",
    )(owned, leave_rows, leave_count)
    arrivals = [swap(packet, link) for packet, link in zip(packets, sides)]

    feats = geometry.reshape(-1, rows_total)
    turned = pl.pallas_call(
        turn_kernel,
        out_shape=jax.ShapeDtypeStruct((rows_total, 2 * feats.shape[0]), BF16),
        in_specs=[VMEM],
        out_specs=VMEM,
        compiler_params=PARAMS,
        name="turn",
    )(feats)

    extended, *sends = pl.pallas_call(
        functools.partial(build_kernel, sides, all_links),
        out_shape=[rows_of(rows_total)] + [rows_of(ghosts)] * len(all_links),
        in_specs=[VMEM] * (2 + len(sides)) + [SMEM],
        out_specs=[VMEM] * (1 + len(all_links)),
        compiler_params=PARAMS,
        name="build",
    )(retained, *arrivals, ghost_list, ghost_total)

    layers = edge_w.shape[0]
    for layer in range(layers):
        last = layer == layers - 1
        landed = [swap(send, link) for send, link in zip(sends, all_links)]
        outs = [rows_of(rows_total)] + ([] if last else [rows_of(ghosts)] * len(all_links))
        extra = [] if last else [ghost_list, ghost_total]
        extended, *sends = pl.pallas_call(
            functools.partial(layer_kernel, layer, last, all_links),
            out_shape=outs,
            in_specs=[VMEM, VMEM, SMEM] + [VMEM] * (5 + len(all_links)) + ([] if last else [VMEM, SMEM]),
            out_specs=[VMEM] * len(outs),
            scratch_shapes=[
                pltpu.VMEM((table_rows, width), F32),
                pltpu.VMEM((turned.shape[1] + width, slots * width), BF16),
                pltpu.VMEM((2 * width, 2 * width), BF16),
                pltpu.VMEM((rows_total, width), F32),
            ],
            compiler_params=PARAMS,
            name="layer",
        )(extended, turned, tile_links, edge_w, node_w, geo_w, biases, gains, *landed, *extra)
    return extended[None, None]


def solution(mesh):
    block = lambda rank: P("gx", "gy", *[None] * rank)
    return jax.shard_map(
        body,
        mesh=mesh,
        in_specs=(block(2), block(2), block(1), block(2), block(1), block(2), block(3), P(), P(), P(), P(), P()),
        out_specs=block(2),
        check_vma=False,
    )
```

```python
import functools
import itertools
import math

import jax
import jax.numpy as jnp
from jax import lax
from jax.experimental import pallas as pl
from jax.experimental.pallas import tpu as pltpu
from jax.sharding import PartitionSpec as P

F32 = jnp.float32
BF16 = jnp.bfloat16
CHUNK = 256
VMEM = pl.BlockSpec(memory_space=pltpu.VMEM)
SMEM = pl.BlockSpec(memory_space=pltpu.SMEM)
HBM = pl.BlockSpec(memory_space=pltpu.HBM)
PARAMS = pltpu.CompilerParams(vmem_limit_bytes=24 * 1024 * 1024)
WHOLE = pltpu.CompilerParams(vmem_limit_bytes=64 * 1024 * 1024)


def partner(place, count, kind):
    other = place + 1 if place % 2 == kind else place - 1
    return other if 0 <= other < count else None


def kinds(count):
    return [0, 1][: max(0, min(2, count - 1))]


def links(count_x, count_y):
    both = itertools.product(kinds(count_x)[::-1] + [None], kinds(count_y)[::-1] + [None])
    return [pair for pair in both if pair != (None, None)]


def swap(value, link):
    count_x, count_y = lax.axis_size("gx"), lax.axis_size("gy")
    pairs = []
    for x, y in itertools.product(range(count_x), range(count_y)):
        to_x = x if link[0] is None else partner(x, count_x, link[0])
        to_y = y if link[1] is None else partner(y, count_y, link[1])
        if to_x is not None and to_y is not None:
            pairs.append((x * count_y + y, to_x * count_y + to_y))
    return lax.ppermute(value, ("gx", "gy"), pairs)


def step(axis, kind):
    if kind is None:
        return 0
    sign = 1 if kind == 0 else -1
    return sign * (1 - 2 * lax.rem(lax.axis_index(axis), 2))


def section(step_x, step_y):
    place = (step_x + 1) * 3 + step_y + 1
    return jnp.where(place > 4, place - 1, place)


def side(link):
    if link[1] is None:
        return (step("gx", link[0]) + 1) // 2
    return 2 + (step("gy", link[1]) + 1) // 2


def fetch(sources, targets, sems):
    copies = [pltpu.make_async_copy(*ends, sems.at[place]) for place, ends in enumerate(zip(sources, targets))]
    for copy in copies:
        copy.start()
    for copy in copies:
        copy.wait()


def fetched(*arrays, smem=()):
    held = [
        (pltpu.SMEM if place in smem else pltpu.VMEM)(array.shape, array.dtype) for place, array in enumerate(arrays)
    ]
    return held + [pltpu.SemaphoreType.DMA((len(arrays),))]


def pack_kernel(sides, latents_hbm, rows_hbm, count_hbm, retained_ref, *refs):
    packet_refs, (latents_ref, rows_ref, count_ref, sems) = refs[: len(sides)], refs[len(sides) :]
    fetch((latents_hbm, rows_hbm, count_hbm), (latents_ref, rows_ref, count_ref), sems)
    total = latents_ref.shape[0]
    slots = rows_ref.shape[1]
    owned = latents_ref[...]
    row_id = lax.broadcasted_iota(jnp.int32, (total, slots), 0)
    lane = lax.broadcasted_iota(jnp.int32, (1, slots), 1)

    def picker(direction):
        wanted = rows_ref[pl.ds(direction, 1), :]
        wanted = jnp.where(lane < count_ref[direction], wanted, -1)
        return (row_id == wanted).astype(F32)

    marks = picker(0)
    for direction in range(1, 4):
        marks = marks + picker(direction)
    marks = jnp.dot(marks.astype(BF16), jnp.ones((slots, owned.shape[1]), BF16), preferred_element_type=F32)
    retained_ref[...] = jnp.where(marks > 0.0, 0.0, owned.astype(F32)).astype(BF16)
    for link, packet_ref in zip(sides, packet_refs):
        chosen = lax.dot_general(
            picker(side(link)).astype(BF16), owned, (((0,), (0,)), ((), ())), preferred_element_type=F32
        )
        packet_ref[...] = chosen.astype(BF16)


def gather_ghosts(extended_ref, wanted_ref, send_refs):
    total = extended_ref.shape[0]
    column = lax.broadcasted_iota(jnp.int32, wanted_ref.shape[1:], 1).astype(F32)
    for place, send_ref in enumerate(send_refs):
        wanted = wanted_ref[place]
        picker = jnp.concatenate(
            [jnp.where(wanted == column + float(start), 1.0, 0.0).astype(BF16) for start in range(0, total, 128)],
            axis=1,
        )
        send_ref[...] = jnp.dot(picker, extended_ref[...], preferred_element_type=F32).astype(BF16)


def build_kernel(sides, retained_ref, *refs):
    arrivals, refs = refs[: len(sides)], refs[len(sides) :]
    wanted_ref, extended_ref, *send_refs = refs
    total = extended_ref.shape[0]
    owned = retained_ref.shape[0]
    slots = (total - owned) // 4
    extended_ref[pl.ds(0, owned), :] = retained_ref[...]
    extended_ref[pl.ds(owned, total - owned), :] = jnp.zeros((total - owned, extended_ref.shape[1]), BF16)
    for link, arrival_ref in zip(sides, arrivals):
        start = pl.multiple_of(owned + slots * side(link), 16)
        extended_ref[pl.ds(start, slots), :] = arrival_ref[...]
    gather_ghosts(extended_ref, wanted_ref, send_refs)


def want_kernel(all_links, rows_ref, count_ref, wanted_ref):
    ghosts = rows_ref.shape[1]
    lane = lax.broadcasted_iota(jnp.int32, (1, ghosts), 1)
    for place, link in enumerate(all_links):
        target = section(step("gx", link[0]), step("gy", link[1]))
        wanted = rows_ref[pl.ds(target, 1), :]
        wanted = jnp.where(lane < count_ref[target], wanted, -1).astype(F32)
        wanted_ref[place] = jnp.transpose(jnp.broadcast_to(wanted, (128, ghosts)))


def static_kernel(geometry_ref, edge_ref, geo_ref, extended_ref, turned_ref, first_ref, second_ref):
    del extended_ref
    feats = geometry_ref[...]
    high = feats.astype(BF16).astype(F32)
    turned_ref[...] = jnp.transpose(jnp.concatenate([high, feats - high], axis=0)).astype(BF16)

    layers, channels, width = geo_ref.shape
    slots = first_ref.shape[2] // width
    part_rows = channels * slots
    slot_of = lax.rem(lax.broadcasted_iota(jnp.int32, (part_rows, width), 0), slots)
    second_ref[...] = jnp.zeros(second_ref.shape, BF16)
    for layer in range(layers):
        spread_geo = jnp.concatenate(
            [jnp.broadcast_to(geo_ref[layer, pl.ds(c, 1), :], (slots, width)) for c in range(channels)], axis=0
        )
        for slot in range(slots):
            part = jnp.where(slot_of == slot, spread_geo, 0.0).astype(BF16)
            columns = pl.ds(slot * width, width)
            first_ref[layer, pl.ds(0, part_rows), columns] = part
            first_ref[layer, pl.ds(part_rows, part_rows), columns] = part
            first_ref[layer, pl.ds(2 * part_rows, width), columns] = edge_ref[layer, 0]
        edge_second = edge_ref[layer, 2].astype(F32)
        edge_second = (edge_second - jnp.mean(edge_second, axis=-1, keepdims=True)).astype(BF16)
        second_ref[layer, pl.ds(0, width), pl.ds(0, width)] = edge_second
        second_ref[layer, pl.ds(width, width), pl.ds(width, width)] = edge_second


def receive_kernel(layer, extended_ref, turned_ref, first_ref, edge_ref, bias_ref, base_ref, table_ref):
    own = jnp.concatenate([turned_ref[...], extended_ref[...]], axis=1)
    width = extended_ref.shape[1]
    bias = bias_ref[layer, pl.ds(0, 1), :]
    bias = jnp.concatenate([bias, bias], axis=1)
    for start in range(0, base_ref.shape[1], 2 * width):
        columns = pl.ds(start, 2 * width)
        base_ref[:, columns] = (jnp.dot(own, first_ref[layer, :, columns], preferred_element_type=F32) + bias).astype(BF16)
    table_ref[...] = jnp.dot(extended_ref[...], edge_ref[layer, 1], preferred_element_type=F32)


def spread_of(center):
    return jnp.sum(center * center, axis=-1, keepdims=True)


def layer_kernel(
    layer, last, all_links, extended_ref, base_ref, own_ref, links_ref, edge_ref, node_ref, second_ref, bias_ref, gain_ref, *refs
):
    landed, refs = refs[: len(all_links)], refs[len(all_links) :]
    if not last:
        wanted_ref, *refs = refs
    updated_ref, *send_refs, table_ref, hidden_ref, total_ref = refs
    rows_total, width = extended_ref.shape
    slots, tiles = links_ref.shape
    rows = rows_total // tiles
    ghosts = landed[0].shape[0]

    sender_mat = edge_ref[layer, 1]
    table_ref[pl.ds(0, rows_total), :] = own_ref[...]
    if len(all_links) < 8:
        table_ref[pl.ds(rows_total, 8 * ghosts), :] = jnp.zeros((8 * ghosts, width), F32)
    for link, landed_ref in zip(all_links, landed):
        source = section(-step("gx", link[0]), -step("gy", link[1]))
        start = pl.multiple_of(rows_total + ghosts * source, 16)
        table_ref[pl.ds(start, ghosts), :] = jnp.dot(landed_ref[...], sender_mat, preferred_element_type=F32)
    bias_second = bias_ref[layer, pl.ds(1, 1), :]
    bias_second = bias_second - jnp.mean(bias_second, axis=-1, keepdims=True)

    chunk_rows = math.gcd(rows_total, CHUNK)
    chunk_tiles = chunk_rows // rows
    chunks = range(0, rows_total, chunk_rows)
    for pair in range(0, slots, 2):
        for start in chunks:
            halves = []
            for slot in (pair, pair + 1):
                senders = []
                for tile in range(start // rows, start // rows + chunk_tiles):
                    picked = table_ref[pl.ds(jnp.maximum(links_ref[slot, tile], 0), 1), :]
                    senders.append(jnp.broadcast_to(picked, (rows, width)))
                halves.append(jnp.concatenate(senders, axis=0))
            base = base_ref[pl.ds(start, chunk_rows), pl.ds(pair * width, 2 * width)].astype(F32)
            hidden = jnp.maximum(base + jnp.concatenate(halves, axis=1), 0.0)
            hidden_ref[pl.ds(start, chunk_rows), :] = hidden.astype(BF16)
        for start in chunks:
            second = jnp.dot(hidden_ref[pl.ds(start, chunk_rows), :], second_ref[layer], preferred_element_type=F32)
            for place in range(0, chunk_rows, rows):
                tile = (start + place) // rows
                total = 0.0 if pair == 0 else total_ref[pl.ds(start + place, rows), :]
                for half in range(2):
                    center = second[place : place + rows, half * width : (half + 1) * width] + bias_second
                    limit = jnp.where(links_ref[pair + half, tile] >= 0, width * 1e-5, jnp.inf)
                    total = total + center * lax.rsqrt(spread_of(center) + limit)
                total_ref[pl.ds(start + place, rows), :] = total

    gathered = (total_ref[...] * (gain_ref[layer, pl.ds(0, 1), :] * math.sqrt(width))).astype(BF16)
    extended = extended_ref[...]
    node_first = jnp.dot(
        jnp.concatenate([extended, gathered], axis=1),
        jnp.concatenate([node_ref[layer, 0], node_ref[layer, 1]], axis=0),
        preferred_element_type=F32,
    )
    node_hidden = jnp.maximum(node_first + bias_ref[layer, pl.ds(2, 1), :], 0.0).astype(BF16)
    node_out = jnp.dot(node_hidden, node_ref[layer, 2], preferred_element_type=F32) + bias_ref[layer, pl.ds(3, 1), :]
    center = node_out - jnp.mean(node_out, axis=-1, keepdims=True)
    scale = lax.rsqrt(spread_of(center) / width + 1e-5)
    updated_ref[...] = (extended.astype(F32) + center * scale * gain_ref[layer, pl.ds(1, 1), :]).astype(BF16)
    if not last:
        gather_ghosts(updated_ref, wanted_ref, send_refs)


def body(
    latents, mig_rows, mig_count, ghost_rows, ghost_count, neighbours, geometry, edge_w, node_w, geo_w, biases, gains
):
    owned = latents[0, 0]
    leave_rows, leave_count = mig_rows[0, 0], mig_count[0, 0]
    ghost_list, ghost_total = ghost_rows[0, 0], ghost_count[0, 0]
    tile_links = neighbours[0, 0]
    width = owned.shape[1]
    slots, tiles = tile_links.shape
    rows_total = geometry.shape[-1]
    ghosts = ghost_list.shape[1]
    table_rows = rows_total + 8 * ghosts
    all_links = links(lax.axis_size("gx"), lax.axis_size("gy"))
    sides = [link for link in all_links if None in link]
    rows_of = lambda count: jax.ShapeDtypeStruct((count, width), BF16)

    retained, *packets = pl.pallas_call(
        functools.partial(pack_kernel, sides),
        out_shape=[rows_of(owned.shape[0])] + [rows_of(leave_rows.shape[1])] * len(sides),
        in_specs=[HBM] * 3,
        out_specs=[VMEM] * (1 + len(sides)),
        scratch_shapes=fetched(owned, leave_rows, leave_count, smem=(2,)),
        compiler_params=WHOLE,
        name="pack",
    )(owned, leave_rows, leave_count)
    arrivals = [swap(packet, link) for packet, link in zip(packets, sides)]

    feats = geometry.reshape(-1, rows_total)
    layers = edge_w.shape[0]
    deep = 2 * feats.shape[0] + width
    wanted = pl.pallas_call(
        functools.partial(want_kernel, all_links),
        out_shape=jax.ShapeDtypeStruct((len(all_links), ghosts, 128), F32),
        in_specs=[VMEM, SMEM],
        out_specs=VMEM,
        compiler_params=PARAMS,
        cost_estimate=pl.CostEstimate(flops=500_000_000, bytes_accessed=1_000_000, transcendentals=0),
        name="want",
    )(ghost_list, ghost_total)
    extended, *sends = pl.pallas_call(
        functools.partial(build_kernel, sides),
        out_shape=[rows_of(rows_total)] + [rows_of(ghosts)] * len(all_links),
        in_specs=[VMEM] * (2 + len(sides)),
        out_specs=[VMEM] * (1 + len(all_links)),
        compiler_params=PARAMS,
        name="build",
    )(retained, *arrivals, wanted)

    turned, first_mats, second_mats = pl.pallas_call(
        static_kernel,
        out_shape=[
            jax.ShapeDtypeStruct((rows_total, 2 * feats.shape[0]), BF16),
            jax.ShapeDtypeStruct((layers, deep, slots * width), BF16),
            jax.ShapeDtypeStruct((layers, 2 * width, 2 * width), BF16),
        ],
        in_specs=[VMEM] * 3 + [pl.BlockSpec(memory_space=pl.ANY)],
        out_specs=[VMEM] * 3,
        compiler_params=PARAMS,
        cost_estimate=pl.CostEstimate(flops=1_000_000_000, bytes_accessed=3_000_000, transcendentals=0),
        name="static",
    )(feats, edge_w, geo_w, extended)

    for layer in range(layers):
        last = layer == layers - 1
        landed = [swap(send, link) for send, link in zip(sends, all_links)]
        base, own = pl.pallas_call(
            functools.partial(receive_kernel, layer),
            out_shape=[
                jax.ShapeDtypeStruct((rows_total, slots * width), BF16),
                jax.ShapeDtypeStruct((rows_total, width), F32),
            ],
            in_specs=[VMEM] * 5,
            out_specs=[VMEM] * 2,
            compiler_params=PARAMS,
            cost_estimate=pl.CostEstimate(flops=2_500_000_000, bytes_accessed=6_000_000, transcendentals=0),
            name="receive",
        )(extended, turned, first_mats, edge_w, biases)
        outs = [rows_of(rows_total)] + ([] if last else [rows_of(ghosts)] * len(all_links))
        extra = [] if last else [wanted]
        extended, *sends = pl.pallas_call(
            functools.partial(layer_kernel, layer, last, all_links),
            out_shape=outs,
            in_specs=[VMEM] * 3 + [SMEM] + [VMEM] * (5 + len(all_links) + len(extra)),
            out_specs=[VMEM] * len(outs),
            scratch_shapes=[
                pltpu.VMEM((table_rows, width), F32),
                pltpu.VMEM((rows_total, 2 * width), BF16),
                pltpu.VMEM((rows_total, width), F32),
            ],
            compiler_params=PARAMS,
            name="layer",
        )(extended, base, own, tile_links, edge_w, node_w, second_mats, biases, gains, *landed, *extra)
    return extended[None, None]


def solution(mesh):
    block = lambda rank: P("gx", "gy", *[None] * rank)
    return jax.shard_map(
        body,
        mesh=mesh,
        in_specs=(block(2), block(2), block(1), block(2), block(1), block(2), block(3), P(), P(), P(), P(), P()),
        out_specs=block(2),
        check_vma=False,
    )
```

```python
import functools
import itertools
import math

import jax
import jax.numpy as jnp
from jax import lax
from jax.experimental import pallas as pl
from jax.experimental.pallas import tpu as pltpu
from jax.sharding import PartitionSpec as P

F32 = jnp.float32
BF16 = jnp.bfloat16
CHUNK = 256
VMEM = pl.BlockSpec(memory_space=pltpu.VMEM)
SMEM = pl.BlockSpec(memory_space=pltpu.SMEM)
HBM = pl.BlockSpec(memory_space=pltpu.HBM)
PARAMS = pltpu.CompilerParams(vmem_limit_bytes=24 * 1024 * 1024)
WHOLE = pltpu.CompilerParams(vmem_limit_bytes=64 * 1024 * 1024)


def partner(place, count, kind):
    other = place + 1 if place % 2 == kind else place - 1
    return other if 0 <= other < count else None


def kinds(count):
    return [0, 1][: max(0, min(2, count - 1))]


def links(count_x, count_y):
    both = itertools.product(kinds(count_x)[::-1] + [None], kinds(count_y)[::-1] + [None])
    return [pair for pair in both if pair != (None, None)]


def messages(all_links):
    along_y = [link for link in all_links if link[0] is None]
    groups = [[(1, None)] + [(1, kind) for _, kind in along_y]] if (1, None) in all_links else []
    groups += [[link, (0, link[1])] for link in along_y]
    return groups + [[(0, None)]]


def exchange(sends, all_links, ghosts):
    landed = {}
    for group, send in zip(messages(all_links), sends):
        arrived = swap(send, group[0])
        for place, link in enumerate(group):
            landed[link] = arrived if place == 0 else arrived[place * ghosts : (place + 1) * ghosts]
    for link in all_links:
        if None not in link:
            landed[link] = swap(landed[link], (None, link[1]) if link[0] == 1 else (0, None))
    return [landed[link] for link in all_links]


def swap(value, link):
    count_x, count_y = lax.axis_size("gx"), lax.axis_size("gy")
    pairs = []
    for x, y in itertools.product(range(count_x), range(count_y)):
        to_x = x if link[0] is None else partner(x, count_x, link[0])
        to_y = y if link[1] is None else partner(y, count_y, link[1])
        if to_x is not None and to_y is not None:
            pairs.append((x * count_y + y, to_x * count_y + to_y))
    return lax.ppermute(value, ("gx", "gy"), pairs)


def step(axis, kind):
    if kind is None:
        return 0
    sign = 1 if kind == 0 else -1
    return sign * (1 - 2 * lax.rem(lax.axis_index(axis), 2))


def section(step_x, step_y):
    place = (step_x + 1) * 3 + step_y + 1
    return jnp.where(place > 4, place - 1, place)


def side(link):
    if link[1] is None:
        return (step("gx", link[0]) + 1) // 2
    return 2 + (step("gy", link[1]) + 1) // 2


def fetch(sources, targets, sems):
    copies = [pltpu.make_async_copy(*ends, sems.at[place]) for place, ends in enumerate(zip(sources, targets))]
    for copy in copies:
        copy.start()
    for copy in copies:
        copy.wait()


def fetched(*arrays, smem=()):
    held = [
        (pltpu.SMEM if place in smem else pltpu.VMEM)(array.shape, array.dtype) for place, array in enumerate(arrays)
    ]
    return held + [pltpu.SemaphoreType.DMA((len(arrays),))]


def pack_kernel(sides, latents_hbm, rows_hbm, count_hbm, retained_ref, *refs):
    packet_refs, (chosen_ref, latents_ref, rows_ref, count_ref, sems) = refs[: len(sides)], refs[len(sides) :]
    fetch((latents_hbm, rows_hbm, count_hbm), (latents_ref, rows_ref, count_ref), sems)
    total = latents_ref.shape[0]
    slots = rows_ref.shape[1]
    owned = latents_ref[...]
    directions = rows_ref.shape[0]
    lane = lax.broadcasted_iota(jnp.int32, (1, slots), 1)
    wanted = jnp.concatenate(
        [jnp.where(lane < count_ref[side_at], rows_ref[pl.ds(side_at, 1), :], -1) for side_at in range(directions)], axis=1
    )
    row_id = lax.broadcasted_iota(jnp.int32, (total, directions * slots), 0)
    picker = (row_id == wanted).astype(F32).astype(BF16)
    chosen = lax.dot_general(picker, owned, (((0,), (0,)), ((), ())), preferred_element_type=F32)
    chosen_ref[...] = chosen.astype(BF16)
    for link, packet_ref in zip(sides, packet_refs):
        packet_ref[...] = chosen_ref[pl.ds(pl.multiple_of(side(link) * slots, 16), slots), :]
    marks = jnp.dot(picker, jnp.ones((directions * slots, owned.shape[1]), BF16), preferred_element_type=F32)
    retained_ref[...] = jnp.where(marks > 0.0, 0.0, owned.astype(F32)).astype(BF16)


def gather_ghosts(extended_ref, wanted_ref, send_refs):
    total = extended_ref.shape[0]
    ghosts = wanted_ref.shape[1]
    spots = [(ref, start) for ref in send_refs for start in range(0, ref.shape[0], ghosts)]
    column = lax.broadcasted_iota(jnp.int32, wanted_ref.shape[1:], 1).astype(F32)
    parts = 2 if total % 256 == 0 else 1
    part = total // parts
    source = jnp.concatenate([extended_ref[pl.ds(start, part), :] for start in range(0, total, part)], axis=1)
    for place, (send_ref, start_row) in enumerate(spots):
        wanted = wanted_ref[place]
        upper = wanted >= float(part)
        within = jnp.where(upper, wanted - float(part), wanted) if parts > 1 else wanted
        picker = jnp.concatenate(
            [jnp.where(within == column + float(start), 1.0, 0.0).astype(BF16) for start in range(0, part, 128)], axis=1
        )
        chosen = jnp.dot(picker, source, preferred_element_type=F32)
        if parts > 1:
            chosen = jnp.where(upper, chosen[:, column.shape[1] :], chosen[:, : column.shape[1]])
        send_ref[pl.ds(start_row, ghosts), :] = chosen.astype(BF16)


def build_kernel(sides, retained_ref, *refs):
    arrivals, refs = refs[: len(sides)], refs[len(sides) :]
    wanted_ref, extended_ref, *send_refs = refs
    total = extended_ref.shape[0]
    owned = retained_ref.shape[0]
    slots = (total - owned) // 4
    extended_ref[pl.ds(0, owned), :] = retained_ref[...]
    extended_ref[pl.ds(owned, total - owned), :] = jnp.zeros((total - owned, extended_ref.shape[1]), BF16)
    for link, arrival_ref in zip(sides, arrivals):
        start = pl.multiple_of(owned + slots * side(link), 16)
        extended_ref[pl.ds(start, slots), :] = arrival_ref[...]
    gather_ghosts(extended_ref, wanted_ref, send_refs)


def want_kernel(order, rows_ref, count_ref, wanted_ref):
    ghosts = rows_ref.shape[1]
    lane = lax.broadcasted_iota(jnp.int32, (1, ghosts), 1)
    for place, link in enumerate(order):
        target = section(step("gx", link[0]), step("gy", link[1]))
        wanted = rows_ref[pl.ds(target, 1), :]
        wanted = jnp.where(lane < count_ref[target], wanted, -1).astype(F32)
        wanted_ref[place] = jnp.transpose(jnp.broadcast_to(wanted, (128, ghosts)))


def static_kernel(geometry_ref, edge_ref, geo_ref, extended_ref, turned_ref, first_ref, second_ref):
    del extended_ref
    feats = geometry_ref[...]
    high = feats.astype(BF16).astype(F32)
    turned_ref[...] = jnp.transpose(jnp.concatenate([high, feats - high], axis=0)).astype(BF16)

    layers, channels, width = geo_ref.shape
    slots = first_ref.shape[2] // width
    part_rows = channels * slots
    slot_of = lax.rem(lax.broadcasted_iota(jnp.int32, (part_rows, width), 0), slots)
    second_ref[...] = jnp.zeros(second_ref.shape, BF16)
    for layer in range(layers):
        spread_geo = jnp.concatenate(
            [jnp.broadcast_to(geo_ref[layer, pl.ds(c, 1), :], (slots, width)) for c in range(channels)], axis=0
        )
        for slot in range(slots):
            part = jnp.where(slot_of == slot, spread_geo, 0.0).astype(BF16)
            columns = pl.ds(slot * width, width)
            first_ref[layer, pl.ds(0, part_rows), columns] = part
            first_ref[layer, pl.ds(part_rows, part_rows), columns] = part
            first_ref[layer, pl.ds(2 * part_rows, width), columns] = edge_ref[layer, 0]
        edge_second = edge_ref[layer, 2].astype(F32)
        edge_second = (edge_second - jnp.mean(edge_second, axis=-1, keepdims=True)).astype(BF16)
        second_ref[layer, pl.ds(0, width), pl.ds(0, width)] = edge_second
        second_ref[layer, pl.ds(width, width), pl.ds(width, width)] = edge_second


def receive_kernel(layer, extended_ref, turned_ref, first_ref, edge_ref, bias_ref, base_ref, table_ref):
    own = jnp.concatenate([turned_ref[...], extended_ref[...]], axis=1)
    width = extended_ref.shape[1]
    bias = bias_ref[layer, pl.ds(0, 1), :]
    bias = jnp.concatenate([bias, bias], axis=1)
    for start in range(0, base_ref.shape[1], 2 * width):
        columns = pl.ds(start, 2 * width)
        base_ref[:, columns] = (jnp.dot(own, first_ref[layer, :, columns], preferred_element_type=F32) + bias).astype(BF16)
    table_ref[...] = jnp.dot(extended_ref[...], edge_ref[layer, 1], preferred_element_type=F32)


def spread_of(center):
    return jnp.sum(center * center, axis=-1, keepdims=True)


def layer_kernel(
    layer, last, ghosts, all_links, extended_ref, base_ref, own_ref, links_ref, edge_ref, node_ref, second_ref, bias_ref, gain_ref, *refs
):
    landed, refs = refs[: len(all_links)], refs[len(all_links) :]
    if not last:
        wanted_ref, *refs = refs
    updated_ref, *send_refs, table_ref, hidden_ref, total_ref = refs
    rows_total, width = extended_ref.shape
    slots, tiles = links_ref.shape
    rows = rows_total // tiles

    sender_mat = edge_ref[layer, 1]
    table_ref[pl.ds(0, rows_total), :] = own_ref[...]
    if len(all_links) < 8:
        table_ref[pl.ds(rows_total, 8 * ghosts), :] = jnp.zeros((8 * ghosts, width), F32)
    for link, landed_ref in zip(all_links, landed):
        source = section(-step("gx", link[0]), -step("gy", link[1]))
        start = pl.multiple_of(rows_total + ghosts * source, 16)
        table_ref[pl.ds(start, ghosts), :] = jnp.dot(landed_ref[pl.ds(0, ghosts), :], sender_mat, preferred_element_type=F32)
    bias_second = bias_ref[layer, pl.ds(1, 1), :]
    bias_second = bias_second - jnp.mean(bias_second, axis=-1, keepdims=True)

    gain_first = gain_ref[layer, pl.ds(0, 1), :] * math.sqrt(width)
    node_mat = jnp.concatenate([node_ref[layer, 0], node_ref[layer, 1]], axis=0)

    def update(start, total):
        extended = extended_ref[pl.ds(start, total.shape[0]), :]
        gathered = (total * gain_first).astype(BF16)
        node_first = jnp.dot(jnp.concatenate([extended, gathered], axis=1), node_mat, preferred_element_type=F32)
        node_hidden = jnp.maximum(node_first + bias_ref[layer, pl.ds(2, 1), :], 0.0).astype(BF16)
        node_out = jnp.dot(node_hidden, node_ref[layer, 2], preferred_element_type=F32)
        node_out = node_out + bias_ref[layer, pl.ds(3, 1), :]
        center = node_out - jnp.mean(node_out, axis=-1, keepdims=True)
        scale = lax.rsqrt(spread_of(center) / width + 1e-5)
        updated = extended.astype(F32) + center * scale * gain_ref[layer, pl.ds(1, 1), :]
        updated_ref[pl.ds(start, total.shape[0]), :] = updated.astype(BF16)

    chunk_rows = math.gcd(rows_total, CHUNK)
    chunk_tiles = chunk_rows // rows
    chunks = range(0, rows_total, chunk_rows)
    for pair in range(0, slots, 2):
        for start in chunks:
            halves = []
            for slot in (pair, pair + 1):
                senders = []
                for tile in range(start // rows, start // rows + chunk_tiles):
                    picked = table_ref[pl.ds(jnp.maximum(links_ref[slot, tile], 0), 1), :]
                    senders.append(jnp.broadcast_to(picked, (rows, width)).astype(BF16))
                halves.append(jnp.concatenate(senders, axis=0))
            base = base_ref[pl.ds(start, chunk_rows), pl.ds(pair * width, 2 * width)]
            hidden_ref[pl.ds(start, chunk_rows), :] = jnp.maximum(base + jnp.concatenate(halves, axis=1), 0)
        for start in chunks:
            second = jnp.dot(hidden_ref[pl.ds(start, chunk_rows), :], second_ref[layer], preferred_element_type=F32)
            for place in range(0, chunk_rows, rows):
                tile = (start + place) // rows
                total = 0.0 if pair == 0 else total_ref[pl.ds(start + place, rows), :]
                for half in range(2):
                    center = second[place : place + rows, half * width : (half + 1) * width] + bias_second
                    limit = jnp.where(links_ref[pair + half, tile] >= 0, width * 1e-5, jnp.inf)
                    total = total + center * lax.rsqrt(spread_of(center) + limit)
                total_ref[pl.ds(start + place, rows), :] = total
    for start in range(0, rows_total, 256):
        update(start, total_ref[pl.ds(start, 256), :])
    if not last:
        gather_ghosts(updated_ref, wanted_ref, send_refs)


def body(
    latents, mig_rows, mig_count, ghost_rows, ghost_count, neighbours, geometry, edge_w, node_w, geo_w, biases, gains
):
    owned = latents[0, 0]
    leave_rows, leave_count = mig_rows[0, 0], mig_count[0, 0]
    ghost_list, ghost_total = ghost_rows[0, 0], ghost_count[0, 0]
    tile_links = neighbours[0, 0]
    width = owned.shape[1]
    slots, tiles = tile_links.shape
    rows_total = geometry.shape[-1]
    ghosts = ghost_list.shape[1]
    table_rows = rows_total + 8 * ghosts
    all_links = links(lax.axis_size("gx"), lax.axis_size("gy"))
    sides = [link for link in all_links if None in link]
    groups = messages(all_links)
    rows_of = lambda count: jax.ShapeDtypeStruct((count, width), BF16)

    retained, *packets = pl.pallas_call(
        functools.partial(pack_kernel, sides),
        out_shape=[rows_of(owned.shape[0])] + [rows_of(leave_rows.shape[1])] * len(sides),
        in_specs=[HBM] * 3,
        out_specs=[VMEM] * (1 + len(sides)),
        scratch_shapes=[pltpu.VMEM((leave_rows.size, width), BF16)] + fetched(owned, leave_rows, leave_count, smem=(2,)),
        compiler_params=WHOLE,
        name="pack",
    )(owned, leave_rows, leave_count)
    arrivals = [swap(packet, link) for packet, link in zip(packets, sides)]

    feats = geometry.reshape(-1, rows_total)
    layers = edge_w.shape[0]
    deep = 2 * feats.shape[0] + width
    wanted = pl.pallas_call(
        functools.partial(want_kernel, sum(groups, [])),
        out_shape=jax.ShapeDtypeStruct((len(all_links), ghosts, 128), F32),
        in_specs=[VMEM, SMEM],
        out_specs=VMEM,
        compiler_params=PARAMS,
        cost_estimate=pl.CostEstimate(flops=500_000_000, bytes_accessed=1_000_000, transcendentals=0),
        name="want",
    )(ghost_list, ghost_total)
    extended, *sends = pl.pallas_call(
        functools.partial(build_kernel, sides),
        out_shape=[rows_of(rows_total)] + [rows_of(ghosts * len(group)) for group in groups],
        in_specs=[VMEM] * (2 + len(sides)),
        out_specs=[VMEM] * (1 + len(groups)),
        compiler_params=PARAMS,
        name="build",
    )(retained, *arrivals, wanted)

    turned, first_mats, second_mats = pl.pallas_call(
        static_kernel,
        out_shape=[
            jax.ShapeDtypeStruct((rows_total, 2 * feats.shape[0]), BF16),
            jax.ShapeDtypeStruct((layers, deep, slots * width), BF16),
            jax.ShapeDtypeStruct((layers, 2 * width, 2 * width), BF16),
        ],
        in_specs=[VMEM] * 3 + [pl.BlockSpec(memory_space=pl.ANY)],
        out_specs=[VMEM] * 3,
        compiler_params=PARAMS,
        cost_estimate=pl.CostEstimate(flops=1_000_000_000, bytes_accessed=3_000_000, transcendentals=0),
        name="static",
    )(feats, edge_w, geo_w, extended)

    for layer in range(layers):
        last = layer == layers - 1
        landed = exchange(sends, all_links, ghosts)
        base, own = pl.pallas_call(
            functools.partial(receive_kernel, layer),
            out_shape=[
                jax.ShapeDtypeStruct((rows_total, slots * width), BF16),
                jax.ShapeDtypeStruct((rows_total, width), F32),
            ],
            in_specs=[VMEM] * 5,
            out_specs=[VMEM] * 2,
            compiler_params=PARAMS,
            cost_estimate=pl.CostEstimate(flops=2_500_000_000, bytes_accessed=6_000_000, transcendentals=0),
            name="receive",
        )(extended, turned, first_mats, edge_w, biases)
        outs = [rows_of(rows_total)] + ([] if last else [rows_of(ghosts * len(group)) for group in groups])
        extra = [] if last else [wanted]
        extended, *sends = pl.pallas_call(
            functools.partial(layer_kernel, layer, last, ghosts, all_links),
            out_shape=outs,
            in_specs=[VMEM] * 3 + [SMEM] + [VMEM] * (5 + len(all_links) + len(extra)),
            out_specs=[VMEM] * len(outs),
            scratch_shapes=[
                pltpu.VMEM((table_rows, width), F32),
                pltpu.VMEM((rows_total, 2 * width), BF16),
                pltpu.VMEM((rows_total, width), F32),
            ],
            compiler_params=PARAMS,
            name="layer",
        )(extended, base, own, tile_links, edge_w, node_w, second_mats, biases, gains, *landed, *extra)
    return extended[None, None]


def solution(mesh):
    block = lambda rank: P("gx", "gy", *[None] * rank)
    return jax.shard_map(
        body,
        mesh=mesh,
        in_specs=(block(2), block(2), block(1), block(2), block(1), block(2), block(3), P(), P(), P(), P(), P()),
        out_specs=block(2),
        check_vma=False,
    )
```

```python
import functools
import itertools
import math

import jax
import jax.numpy as jnp
from jax import lax
from jax.experimental import pallas as pl
from jax.experimental.pallas import tpu as pltpu
from jax.sharding import PartitionSpec as P

F32 = jnp.float32
BF16 = jnp.bfloat16
CHUNK = 256
VMEM = pl.BlockSpec(memory_space=pltpu.VMEM)
SMEM = pl.BlockSpec(memory_space=pltpu.SMEM)
HBM = pl.BlockSpec(memory_space=pltpu.HBM)
PARAMS = pltpu.CompilerParams(vmem_limit_bytes=24 * 1024 * 1024)
WHOLE = pltpu.CompilerParams(vmem_limit_bytes=64 * 1024 * 1024)


def partner(place, count, kind):
    other = place + 1 if place % 2 == kind else place - 1
    return other if 0 <= other < count else None


def kinds(count):
    return [0, 1][: max(0, min(2, count - 1))]


def links(count_x, count_y):
    both = itertools.product(kinds(count_x)[::-1] + [None], kinds(count_y)[::-1] + [None])
    return [pair for pair in both if pair != (None, None)]


def messages(all_links):
    along_y = [link for link in all_links if link[0] is None]
    groups = [[(1, None)] + [(1, kind) for _, kind in along_y]] if (1, None) in all_links else []
    groups += [[link, (0, link[1])] for link in along_y]
    return groups + [[(0, None)]]


def exchange(sends, all_links, ghosts):
    landed = {}
    for group, send in zip(messages(all_links), sends):
        arrived = swap(send, group[0])
        for place, link in enumerate(group):
            landed[link] = arrived if place == 0 else arrived[place * ghosts : (place + 1) * ghosts]
    for link in all_links:
        if None not in link:
            landed[link] = swap(landed[link], (None, link[1]) if link[0] == 1 else (0, None))
    return [landed[link] for link in all_links]


def swap(value, link):
    count_x, count_y = lax.axis_size("gx"), lax.axis_size("gy")
    pairs = []
    for x, y in itertools.product(range(count_x), range(count_y)):
        to_x = x if link[0] is None else partner(x, count_x, link[0])
        to_y = y if link[1] is None else partner(y, count_y, link[1])
        if to_x is not None and to_y is not None:
            pairs.append((x * count_y + y, to_x * count_y + to_y))
    return lax.ppermute(value, ("gx", "gy"), pairs)


def step(axis, kind):
    if kind is None:
        return 0
    sign = 1 if kind == 0 else -1
    return sign * (1 - 2 * lax.rem(lax.axis_index(axis), 2))


def section(step_x, step_y):
    place = (step_x + 1) * 3 + step_y + 1
    return jnp.where(place > 4, place - 1, place)


def side(link):
    if link[1] is None:
        return (step("gx", link[0]) + 1) // 2
    return 2 + (step("gy", link[1]) + 1) // 2


def fetch(sources, targets, sems):
    copies = [pltpu.make_async_copy(*ends, sems.at[place]) for place, ends in enumerate(zip(sources, targets))]
    for copy in copies:
        copy.start()
    for copy in copies:
        copy.wait()


def fetched(*arrays, smem=()):
    held = [
        (pltpu.SMEM if place in smem else pltpu.VMEM)(array.shape, array.dtype) for place, array in enumerate(arrays)
    ]
    return held + [pltpu.SemaphoreType.DMA((len(arrays),))]


def pack_kernel(sides, latents_hbm, rows_hbm, count_hbm, retained_ref, *refs):
    packet_refs, (chosen_ref, latents_ref, rows_ref, count_ref, sems) = refs[: len(sides)], refs[len(sides) :]
    fetch((latents_hbm, rows_hbm, count_hbm), (latents_ref, rows_ref, count_ref), sems)
    total = latents_ref.shape[0]
    slots = rows_ref.shape[1]
    owned = latents_ref[...]
    directions = rows_ref.shape[0]
    lane = lax.broadcasted_iota(jnp.int32, (1, slots), 1)
    wanted = jnp.concatenate(
        [jnp.where(lane < count_ref[side_at], rows_ref[pl.ds(side_at, 1), :], -1) for side_at in range(directions)], axis=1
    )
    row_id = lax.broadcasted_iota(jnp.int32, (total, directions * slots), 0)
    picker = (row_id == wanted).astype(F32).astype(BF16)
    chosen = lax.dot_general(picker, owned, (((0,), (0,)), ((), ())), preferred_element_type=F32)
    chosen_ref[...] = chosen.astype(BF16)
    for link, packet_ref in zip(sides, packet_refs):
        packet_ref[...] = chosen_ref[pl.ds(pl.multiple_of(side(link) * slots, 16), slots), :]
    marks = jnp.dot(picker, jnp.ones((directions * slots, owned.shape[1]), BF16), preferred_element_type=F32)
    retained_ref[...] = jnp.where(marks > 0.0, 0.0, owned.astype(F32)).astype(BF16)


def gather_ghosts(extended_ref, wanted_ref, send_refs):
    total = extended_ref.shape[0]
    ghosts = wanted_ref.shape[1]
    spots = [(ref, start) for ref in send_refs for start in range(0, ref.shape[0], ghosts)]
    column = lax.broadcasted_iota(jnp.int32, wanted_ref.shape[1:], 1).astype(F32)
    parts = 2 if total % 256 == 0 else 1
    part = total // parts
    source = jnp.concatenate([extended_ref[pl.ds(start, part), :] for start in range(0, total, part)], axis=1)
    for place, (send_ref, start_row) in enumerate(spots):
        wanted = wanted_ref[place]
        upper = wanted >= float(part)
        within = jnp.where(upper, wanted - float(part), wanted) if parts > 1 else wanted
        picker = jnp.concatenate(
            [jnp.where(within == column + float(start), 1.0, 0.0).astype(BF16) for start in range(0, part, 128)], axis=1
        )
        chosen = jnp.dot(picker, source, preferred_element_type=F32)
        if parts > 1:
            chosen = jnp.where(upper, chosen[:, column.shape[1] :], chosen[:, : column.shape[1]])
        send_ref[pl.ds(start_row, ghosts), :] = chosen.astype(BF16)


def build_kernel(sides, retained_ref, *refs):
    arrivals, refs = refs[: len(sides)], refs[len(sides) :]
    wanted_ref, extended_ref, *send_refs = refs
    total = extended_ref.shape[0]
    owned = retained_ref.shape[0]
    slots = (total - owned) // 4
    extended_ref[pl.ds(0, owned), :] = retained_ref[...]
    extended_ref[pl.ds(owned, total - owned), :] = jnp.zeros((total - owned, extended_ref.shape[1]), BF16)
    for link, arrival_ref in zip(sides, arrivals):
        start = pl.multiple_of(owned + slots * side(link), 16)
        extended_ref[pl.ds(start, slots), :] = arrival_ref[...]
    gather_ghosts(extended_ref, wanted_ref, send_refs)


def want_kernel(order, rows_ref, retained_ref, wanted_ref, kept_ref):
    ghosts = rows_ref.shape[1]
    kept_ref[...] = retained_ref[...]
    for place, link in enumerate(order):
        target = section(step("gx", link[0]), step("gy", link[1]))
        wanted = rows_ref[pl.ds(target, 1), :].astype(F32)
        wanted_ref[place] = jnp.transpose(jnp.broadcast_to(wanted, (128, ghosts)))


def static_kernel(geometry_ref, edge_ref, geo_ref, extended_ref, turned_ref, first_ref, second_ref):
    del extended_ref
    feats = geometry_ref[...]
    high = feats.astype(BF16).astype(F32)
    turned_ref[...] = jnp.transpose(jnp.concatenate([high, feats - high], axis=0)).astype(BF16)

    layers, channels, width = geo_ref.shape
    slots = first_ref.shape[2] // width
    part_rows = channels * slots
    slot_of = lax.rem(lax.broadcasted_iota(jnp.int32, (part_rows, width), 0), slots)
    second_ref[...] = jnp.zeros(second_ref.shape, BF16)
    for layer in range(layers):
        spread_geo = jnp.concatenate(
            [jnp.broadcast_to(geo_ref[layer, pl.ds(c, 1), :], (slots, width)) for c in range(channels)], axis=0
        )
        for slot in range(slots):
            part = jnp.where(slot_of == slot, spread_geo, 0.0).astype(BF16)
            columns = pl.ds(slot * width, width)
            first_ref[layer, pl.ds(0, part_rows), columns] = part
            first_ref[layer, pl.ds(part_rows, part_rows), columns] = part
            first_ref[layer, pl.ds(2 * part_rows, width), columns] = edge_ref[layer, 0]
        edge_second = edge_ref[layer, 2].astype(F32)
        edge_second = (edge_second - jnp.mean(edge_second, axis=-1, keepdims=True)).astype(BF16)
        second_ref[layer, pl.ds(0, width), pl.ds(0, width)] = edge_second
        second_ref[layer, pl.ds(width, width), pl.ds(width, width)] = edge_second


def receive_kernel(layer, extended_ref, turned_ref, first_ref, edge_ref, bias_ref, base_ref, table_ref):
    own = jnp.concatenate([turned_ref[...], extended_ref[...]], axis=1)
    width = extended_ref.shape[1]
    bias = bias_ref[layer, pl.ds(0, 1), :]
    bias = jnp.concatenate([bias, bias], axis=1)
    for start in range(0, base_ref.shape[1], 2 * width):
        columns = pl.ds(start, 2 * width)
        base_ref[:, columns] = (jnp.dot(own, first_ref[layer, :, columns], preferred_element_type=F32) + bias).astype(BF16)
    table_ref[...] = jnp.dot(extended_ref[...], edge_ref[layer, 1], preferred_element_type=F32)


def spread_of(center):
    return jnp.sum(center * center, axis=-1, keepdims=True)


def layer_kernel(
    layer, last, ghosts, all_links, extended_ref, base_ref, own_ref, links_ref, edge_ref, node_ref, second_ref, bias_ref, gain_ref, *refs
):
    landed, refs = refs[: len(all_links)], refs[len(all_links) :]
    if not last:
        wanted_ref, *refs = refs
    updated_ref, *send_refs, table_ref, hidden_ref, total_ref = refs
    rows_total, width = extended_ref.shape
    slots, tiles = links_ref.shape
    rows = rows_total // tiles

    sender_mat = edge_ref[layer, 1]
    table_ref[pl.ds(0, rows_total), :] = own_ref[...]
    if len(all_links) < 8:
        table_ref[pl.ds(rows_total, 8 * ghosts), :] = jnp.zeros((8 * ghosts, width), F32)
    for link, landed_ref in zip(all_links, landed):
        source = section(-step("gx", link[0]), -step("gy", link[1]))
        start = pl.multiple_of(rows_total + ghosts * source, 16)
        table_ref[pl.ds(start, ghosts), :] = jnp.dot(landed_ref[pl.ds(0, ghosts), :], sender_mat, preferred_element_type=F32)
    bias_second = bias_ref[layer, pl.ds(1, 1), :]
    bias_second = bias_second - jnp.mean(bias_second, axis=-1, keepdims=True)

    gain_first = gain_ref[layer, pl.ds(0, 1), :] * math.sqrt(width)
    node_mat = jnp.concatenate([node_ref[layer, 0], node_ref[layer, 1]], axis=0)

    def update(start, total):
        extended = extended_ref[pl.ds(start, total.shape[0]), :]
        gathered = (total * gain_first).astype(BF16)
        node_first = jnp.dot(jnp.concatenate([extended, gathered], axis=1), node_mat, preferred_element_type=F32)
        node_hidden = jnp.maximum(node_first + bias_ref[layer, pl.ds(2, 1), :], 0.0).astype(BF16)
        node_out = jnp.dot(node_hidden, node_ref[layer, 2], preferred_element_type=F32)
        node_out = node_out + bias_ref[layer, pl.ds(3, 1), :]
        center = node_out - jnp.mean(node_out, axis=-1, keepdims=True)
        scale = lax.rsqrt(spread_of(center) / width + 1e-5)
        updated = extended.astype(F32) + center * scale * gain_ref[layer, pl.ds(1, 1), :]
        updated_ref[pl.ds(start, total.shape[0]), :] = updated.astype(BF16)

    chunk_rows = math.gcd(rows_total, CHUNK)
    chunk_tiles = chunk_rows // rows
    chunks = range(0, rows_total, chunk_rows)
    for pair in range(0, slots, 2):
        for start in chunks:
            halves = []
            for slot in (pair, pair + 1):
                senders = []
                for tile in range(start // rows, start // rows + chunk_tiles):
                    picked = table_ref[pl.ds(jnp.maximum(links_ref[slot, tile], 0), 1), :]
                    senders.append(jnp.broadcast_to(picked, (rows, width)).astype(BF16))
                halves.append(jnp.concatenate(senders, axis=0))
            base = base_ref[pl.ds(start, chunk_rows), pl.ds(pair * width, 2 * width)]
            hidden_ref[pl.ds(start, chunk_rows), :] = jnp.maximum(base + jnp.concatenate(halves, axis=1), 0)
        for start in chunks:
            second = jnp.dot(hidden_ref[pl.ds(start, chunk_rows), :], second_ref[layer], preferred_element_type=F32)
            for place in range(0, chunk_rows, rows):
                tile = (start + place) // rows
                total = 0.0 if pair == 0 else total_ref[pl.ds(start + place, rows), :]
                for half in range(2):
                    center = second[place : place + rows, half * width : (half + 1) * width] + bias_second
                    limit = jnp.where(links_ref[pair + half, tile] >= 0, width * 1e-5, jnp.inf)
                    total = total + center * lax.rsqrt(spread_of(center) + limit)
                total_ref[pl.ds(start + place, rows), :] = total
    for start in range(0, rows_total, 256):
        update(start, total_ref[pl.ds(start, 256), :])
    if not last:
        gather_ghosts(updated_ref, wanted_ref, send_refs)


def body(
    latents, mig_rows, mig_count, ghost_rows, ghost_count, neighbours, geometry, edge_w, node_w, geo_w, biases, gains
):
    owned = latents[0, 0]
    leave_rows, leave_count = mig_rows[0, 0], mig_count[0, 0]
    ghost_list, ghost_total = ghost_rows[0, 0], ghost_count[0, 0]
    tile_links = neighbours[0, 0]
    width = owned.shape[1]
    slots, tiles = tile_links.shape
    rows_total = geometry.shape[-1]
    ghosts = ghost_list.shape[1]
    table_rows = rows_total + 8 * ghosts
    all_links = links(lax.axis_size("gx"), lax.axis_size("gy"))
    sides = [link for link in all_links if None in link]
    groups = messages(all_links)
    rows_of = lambda count: jax.ShapeDtypeStruct((count, width), BF16)

    retained, *packets = pl.pallas_call(
        functools.partial(pack_kernel, sides),
        out_shape=[rows_of(owned.shape[0])] + [rows_of(leave_rows.shape[1])] * len(sides),
        in_specs=[HBM] * 3,
        out_specs=[VMEM] * (1 + len(sides)),
        scratch_shapes=[pltpu.VMEM((leave_rows.size, width), BF16)] + fetched(owned, leave_rows, leave_count, smem=(2,)),
        compiler_params=WHOLE,
        name="pack",
    )(owned, leave_rows, leave_count)
    arrivals = [swap(packet, link) for packet, link in zip(packets, sides)]

    feats = geometry.reshape(-1, rows_total)
    layers = edge_w.shape[0]
    deep = 2 * feats.shape[0] + width
    valid_ghosts = jnp.where(jnp.arange(ghosts)[None, :] < ghost_total[:, None], ghost_list, -1)
    wanted, kept = pl.pallas_call(
        functools.partial(want_kernel, sum(groups, [])),
        out_shape=[jax.ShapeDtypeStruct((len(all_links), ghosts, 128), F32), rows_of(owned.shape[0])],
        in_specs=[VMEM] * 2,
        out_specs=[VMEM] * 2,
        compiler_params=PARAMS,
        cost_estimate=pl.CostEstimate(flops=500_000_000, bytes_accessed=1_000_000, transcendentals=0),
        name="want",
    )(valid_ghosts, retained)

    extended, *sends = pl.pallas_call(
        functools.partial(build_kernel, sides),
        out_shape=[rows_of(rows_total)] + [rows_of(ghosts * len(group)) for group in groups],
        in_specs=[VMEM] * (2 + len(sides)),
        out_specs=[VMEM] * (1 + len(groups)),
        compiler_params=PARAMS,
        name="build",
    )(kept, *arrivals, wanted)

    turned, first_mats, second_mats = pl.pallas_call(
        static_kernel,
        out_shape=[
            jax.ShapeDtypeStruct((rows_total, 2 * feats.shape[0]), BF16),
            jax.ShapeDtypeStruct((layers, deep, slots * width), BF16),
            jax.ShapeDtypeStruct((layers, 2 * width, 2 * width), BF16),
        ],
        in_specs=[VMEM] * 3 + [pl.BlockSpec(memory_space=pl.ANY)],
        out_specs=[VMEM] * 3,
        compiler_params=PARAMS,
        cost_estimate=pl.CostEstimate(flops=1_000_000_000, bytes_accessed=3_000_000, transcendentals=0),
        name="static",
    )(feats, edge_w, geo_w, extended)

    for layer in range(layers):
        last = layer == layers - 1
        landed = exchange(sends, all_links, ghosts)
        base, own = pl.pallas_call(
            functools.partial(receive_kernel, layer),
            out_shape=[
                jax.ShapeDtypeStruct((rows_total, slots * width), BF16),
                jax.ShapeDtypeStruct((rows_total, width), F32),
            ],
            in_specs=[VMEM] * 5,
            out_specs=[VMEM] * 2,
            compiler_params=PARAMS,
            cost_estimate=pl.CostEstimate(flops=2_500_000_000, bytes_accessed=6_000_000, transcendentals=0),
            name="receive",
        )(extended, turned, first_mats, edge_w, biases)
        outs = [rows_of(rows_total)] + ([] if last else [rows_of(ghosts * len(group)) for group in groups])
        extra = [] if last else [wanted]
        extended, *sends = pl.pallas_call(
            functools.partial(layer_kernel, layer, last, ghosts, all_links),
            out_shape=outs,
            in_specs=[VMEM] * 3 + [SMEM] + [VMEM] * (5 + len(all_links) + len(extra)),
            out_specs=[VMEM] * len(outs),
            scratch_shapes=[
                pltpu.VMEM((table_rows, width), F32),
                pltpu.VMEM((rows_total, 2 * width), BF16),
                pltpu.VMEM((rows_total, width), F32),
            ],
            compiler_params=PARAMS,
            name="layer",
        )(extended, base, own, tile_links, edge_w, node_w, second_mats, biases, gains, *landed, *extra)
    return extended[None, None]


def solution(mesh):
    block = lambda rank: P("gx", "gy", *[None] * rank)
    return jax.shard_map(
        body,
        mesh=mesh,
        in_specs=(block(2), block(2), block(1), block(2), block(1), block(2), block(3), P(), P(), P(), P(), P()),
        out_specs=block(2),
        check_vma=False,
    )
```

```python
import functools
import itertools
import math

import jax
import jax.numpy as jnp
from jax import lax
from jax.experimental import pallas as pl
from jax.experimental.pallas import tpu as pltpu
from jax.sharding import PartitionSpec as P

F32 = jnp.float32
BF16 = jnp.bfloat16
CHUNK = 1280
NOTHING = -1e30
VMEM = pl.BlockSpec(memory_space=pltpu.VMEM)
SMEM = pl.BlockSpec(memory_space=pltpu.SMEM)
HBM = pl.BlockSpec(memory_space=pltpu.HBM)
PARAMS = pltpu.CompilerParams(vmem_limit_bytes=24 * 1024 * 1024)
WHOLE = pltpu.CompilerParams(vmem_limit_bytes=64 * 1024 * 1024)


def partner(place, count, kind):
    other = place + 1 if place % 2 == kind else place - 1
    return other if 0 <= other < count else None


def kinds(count):
    return [0, 1][: max(0, min(2, count - 1))]


def links(count_x, count_y):
    both = itertools.product(kinds(count_x)[::-1] + [None], kinds(count_y)[::-1] + [None])
    return [pair for pair in both if pair != (None, None)]


def messages(all_links):
    along_y = [link for link in all_links if link[0] is None]
    groups = [[(1, None)] + [(1, kind) for _, kind in along_y]] if (1, None) in all_links else []
    groups += [[link, (0, link[1])] for link in along_y]
    return groups + [[(0, None)]]


def exchange(sends, all_links, ghosts):
    landed = {}
    for group, send in zip(messages(all_links), sends):
        arrived = swap(send, group[0])
        for place, link in enumerate(group):
            landed[link] = arrived if place == 0 else arrived[place * ghosts : (place + 1) * ghosts]
    for link in all_links:
        if None not in link:
            landed[link] = swap(landed[link], (None, link[1]) if link[0] == 1 else (0, None))
    return [landed[link] for link in all_links]


def swap(value, link):
    count_x, count_y = lax.axis_size("gx"), lax.axis_size("gy")
    pairs = []
    for x, y in itertools.product(range(count_x), range(count_y)):
        to_x = x if link[0] is None else partner(x, count_x, link[0])
        to_y = y if link[1] is None else partner(y, count_y, link[1])
        if to_x is not None and to_y is not None:
            pairs.append((x * count_y + y, to_x * count_y + to_y))
    return lax.ppermute(value, ("gx", "gy"), pairs)


def step(axis, kind):
    if kind is None:
        return 0
    sign = 1 if kind == 0 else -1
    return sign * (1 - 2 * lax.rem(lax.axis_index(axis), 2))


def section(step_x, step_y):
    place = (step_x + 1) * 3 + step_y + 1
    return jnp.where(place > 4, place - 1, place)


def side(link):
    if link[1] is None:
        return (step("gx", link[0]) + 1) // 2
    return 2 + (step("gy", link[1]) + 1) // 2


def fetch(sources, targets, sems):
    copies = [pltpu.make_async_copy(*ends, sems.at[place]) for place, ends in enumerate(zip(sources, targets))]
    for copy in copies:
        copy.start()
    for copy in copies:
        copy.wait()


def fetched(*arrays, smem=()):
    held = [
        (pltpu.SMEM if place in smem else pltpu.VMEM)(array.shape, array.dtype) for place, array in enumerate(arrays)
    ]
    return held + [pltpu.SemaphoreType.DMA((len(arrays),))]


def pack_kernel(sides, latents_hbm, rows_hbm, count_hbm, retained_ref, *refs):
    packet_refs, (chosen_ref, latents_ref, rows_ref, count_ref, sems) = refs[: len(sides)], refs[len(sides) :]
    fetch((latents_hbm, rows_hbm, count_hbm), (latents_ref, rows_ref, count_ref), sems)
    total = latents_ref.shape[0]
    slots = rows_ref.shape[1]
    owned = latents_ref[...]
    directions = rows_ref.shape[0]
    lane = lax.broadcasted_iota(jnp.int32, (1, slots), 1)
    wanted = jnp.concatenate(
        [jnp.where(lane < count_ref[side_at], rows_ref[pl.ds(side_at, 1), :], -1) for side_at in range(directions)], axis=1
    )
    row_id = lax.broadcasted_iota(jnp.int32, (total, directions * slots), 0)
    picker = (row_id == wanted).astype(F32).astype(BF16)
    chosen = lax.dot_general(picker, owned, (((0,), (0,)), ((), ())), preferred_element_type=F32)
    chosen_ref[...] = chosen.astype(BF16)
    for link, packet_ref in zip(sides, packet_refs):
        packet_ref[...] = chosen_ref[pl.ds(pl.multiple_of(side(link) * slots, 16), slots), :]
    marks = jnp.dot(picker, jnp.ones((directions * slots, owned.shape[1]), BF16), preferred_element_type=F32)
    retained_ref[...] = jnp.where(marks > 0.0, 0.0, owned.astype(F32)).astype(BF16)


def gather_ghosts(extended_ref, wanted_ref, send_refs):
    total = extended_ref.shape[0]
    ghosts = wanted_ref.shape[1]
    spots = [(ref, start) for ref in send_refs for start in range(0, ref.shape[0], ghosts)]
    column = lax.broadcasted_iota(jnp.int32, wanted_ref.shape[1:], 1).astype(F32)
    parts = 2 if total % 256 == 0 else 1
    part = total // parts
    source = jnp.concatenate([extended_ref[pl.ds(start, part), :] for start in range(0, total, part)], axis=1)
    for place, (send_ref, start_row) in enumerate(spots):
        wanted = wanted_ref[place]
        upper = wanted >= float(part)
        within = jnp.where(upper, wanted - float(part), wanted) if parts > 1 else wanted
        picker = jnp.concatenate(
            [jnp.where(within == column + float(start), 1.0, 0.0).astype(BF16) for start in range(0, part, 128)], axis=1
        )
        chosen = jnp.dot(picker, source, preferred_element_type=F32)
        if parts > 1:
            chosen = jnp.where(upper, chosen[:, column.shape[1] :], chosen[:, : column.shape[1]])
        send_ref[pl.ds(start_row, ghosts), :] = chosen.astype(BF16)


def build_kernel(sides, retained_ref, *refs):
    arrivals, refs = refs[: len(sides)], refs[len(sides) :]
    wanted_ref, extended_ref, *send_refs = refs
    total = extended_ref.shape[0]
    owned = retained_ref.shape[0]
    slots = (total - owned) // 4
    extended_ref[pl.ds(0, owned), :] = retained_ref[...]
    extended_ref[pl.ds(owned, total - owned), :] = jnp.zeros((total - owned, extended_ref.shape[1]), BF16)
    for link, arrival_ref in zip(sides, arrivals):
        start = pl.multiple_of(owned + slots * side(link), 16)
        extended_ref[pl.ds(start, slots), :] = arrival_ref[...]
    gather_ghosts(extended_ref, wanted_ref, send_refs)


def want_kernel(order, rows_ref, retained_ref, wanted_ref, kept_ref):
    ghosts = rows_ref.shape[1]
    kept_ref[...] = retained_ref[...]
    for place, link in enumerate(order):
        target = section(step("gx", link[0]), step("gy", link[1]))
        wanted = rows_ref[pl.ds(target, 1), :].astype(F32)
        wanted_ref[place] = jnp.transpose(jnp.broadcast_to(wanted, (128, ghosts)))


def static_kernel(geometry_ref, edge_ref, geo_ref, extended_ref, turned_ref, first_ref, second_ref):
    del extended_ref
    feats = geometry_ref[...]
    high = feats.astype(BF16).astype(F32)
    turned_ref[...] = jnp.transpose(jnp.concatenate([high, feats - high], axis=0)).astype(BF16)

    layers, channels, width = geo_ref.shape
    slots = first_ref.shape[2] // width
    part_rows = channels * slots
    slot_of = lax.rem(lax.broadcasted_iota(jnp.int32, (part_rows, width), 0), slots)
    second_ref[...] = jnp.zeros(second_ref.shape, BF16)
    for layer in range(layers):
        spread_geo = jnp.concatenate(
            [jnp.broadcast_to(geo_ref[layer, pl.ds(c, 1), :], (slots, width)) for c in range(channels)], axis=0
        )
        for slot in range(slots):
            part = jnp.where(slot_of == slot, spread_geo, 0.0).astype(BF16)
            columns = pl.ds(slot * width, width)
            first_ref[layer, pl.ds(0, part_rows), columns] = part
            first_ref[layer, pl.ds(part_rows, part_rows), columns] = part
            first_ref[layer, pl.ds(2 * part_rows, width), columns] = edge_ref[layer, 0]
        edge_second = edge_ref[layer, 2].astype(F32)
        edge_second = (edge_second - jnp.mean(edge_second, axis=-1, keepdims=True)).astype(BF16)
        second_ref[layer, pl.ds(0, width), pl.ds(0, width)] = edge_second
        second_ref[layer, pl.ds(width, width), pl.ds(width, width)] = edge_second


def receive_kernel(layer, extended_ref, turned_ref, first_ref, edge_ref, bias_ref, links_ref, base_ref, table_ref, empty_ref):
    own = jnp.concatenate([turned_ref[...], extended_ref[...]], axis=1)
    width = extended_ref.shape[1]
    bias = bias_ref[layer, pl.ds(0, 1), :]
    bias = jnp.concatenate([bias, bias], axis=1)
    for start in range(0, base_ref.shape[1], 2 * width):
        columns = pl.ds(start, 2 * width)
        base_ref[:, columns] = (jnp.dot(own, first_ref[layer, :, columns], preferred_element_type=F32) + bias).astype(BF16)
    table_ref[...] = jnp.dot(extended_ref[...], edge_ref[layer, 1], preferred_element_type=F32)
    slots, tiles = links_ref.shape
    rows_total = extended_ref.shape[0]
    vacant = jnp.where(links_ref[...] < 0, 1.0, 0.0).astype(BF16)
    counts = lax.dot_general(
        vacant, jnp.ones((slots, width), BF16), (((0,), (0,)), ((), ())), preferred_element_type=F32
    ).astype(BF16)
    tile_of = lax.div(lax.broadcasted_iota(jnp.int32, (rows_total, tiles), 0), rows_total // tiles)
    spread = (tile_of == lax.broadcasted_iota(jnp.int32, (rows_total, tiles), 1)).astype(F32).astype(BF16)
    empty_ref[...] = jnp.dot(spread, counts, preferred_element_type=F32)


def spread_of(center):
    return jnp.sum(center * center, axis=-1, keepdims=True)


def layer_kernel(
    layer, last, ghosts, all_links, extended_ref, base_ref, own_ref, empty_ref, links_ref, edge_ref, node_ref, second_ref, bias_ref, gain_ref, *refs
):
    landed, refs = refs[: len(all_links)], refs[len(all_links) :]
    if not last:
        wanted_ref, *refs = refs
    updated_ref, *send_refs, table_ref, hidden_ref, total_ref = refs
    rows_total, width = extended_ref.shape
    slots, tiles = links_ref.shape
    rows = rows_total // tiles

    sender_mat = edge_ref[layer, 1]
    table_rows = rows_total + 8 * ghosts
    table_ref[pl.ds(table_rows, 8), :] = jnp.full((8, width), NOTHING, F32)
    table_ref[pl.ds(0, rows_total), :] = own_ref[...]
    if len(all_links) < 8:
        table_ref[pl.ds(rows_total, 8 * ghosts), :] = jnp.zeros((8 * ghosts, width), F32)
    for link, landed_ref in zip(all_links, landed):
        source = section(-step("gx", link[0]), -step("gy", link[1]))
        start = pl.multiple_of(rows_total + ghosts * source, 16)
        table_ref[pl.ds(start, ghosts), :] = jnp.dot(landed_ref[pl.ds(0, ghosts), :], sender_mat, preferred_element_type=F32)
    bias_second = bias_ref[layer, pl.ds(1, 1), :]
    bias_second = bias_second - jnp.mean(bias_second, axis=-1, keepdims=True)

    empty_message = -bias_second * lax.rsqrt(spread_of(bias_second) + width * 1e-5)
    gain_first = gain_ref[layer, pl.ds(0, 1), :] * math.sqrt(width)
    node_mat = jnp.concatenate([node_ref[layer, 0], node_ref[layer, 1]], axis=0)

    def update(start, total):
        extended = extended_ref[pl.ds(start, total.shape[0]), :]
        gathered = (total * gain_first).astype(BF16)
        node_first = jnp.dot(jnp.concatenate([extended, gathered], axis=1), node_mat, preferred_element_type=F32)
        node_hidden = jnp.maximum(node_first + bias_ref[layer, pl.ds(2, 1), :], 0.0).astype(BF16)
        node_out = jnp.dot(node_hidden, node_ref[layer, 2], preferred_element_type=F32)
        node_out = node_out + bias_ref[layer, pl.ds(3, 1), :]
        center = node_out - jnp.mean(node_out, axis=-1, keepdims=True)
        scale = lax.rsqrt(spread_of(center) / width + 1e-5)
        updated = extended.astype(F32) + center * scale * gain_ref[layer, pl.ds(1, 1), :]
        updated_ref[pl.ds(start, total.shape[0]), :] = updated.astype(BF16)

    chunk_rows = math.gcd(rows_total, CHUNK)
    chunk_tiles = chunk_rows // rows
    chunks = range(0, rows_total, chunk_rows)
    for pair in range(0, slots, 2):
        for start in chunks:
            halves = []
            for slot in (pair, pair + 1):
                senders = []
                for tile in range(start // rows, start // rows + chunk_tiles):
                    row = links_ref[slot, tile]
                    picked = table_ref[pl.ds(jnp.where(row >= 0, row, table_rows), 1), :]
                    senders.append(jnp.broadcast_to(picked, (rows, width)).astype(BF16))
                halves.append(jnp.concatenate(senders, axis=0))
            base = base_ref[pl.ds(start, chunk_rows), pl.ds(pair * width, 2 * width)]
            hidden_ref[pl.ds(start, chunk_rows), :] = jnp.maximum(base + jnp.concatenate(halves, axis=1), 0)
        for start in chunks:
            second = jnp.dot(hidden_ref[pl.ds(start, chunk_rows), :], second_ref[layer], preferred_element_type=F32)
            for place in range(0, chunk_rows, rows):
                spot = pl.ds(start + place, rows)
                total = empty_ref[spot, :] * empty_message if pair == 0 else total_ref[spot, :]
                for half in range(2):
                    center = second[place : place + rows, half * width : (half + 1) * width] + bias_second
                    total = total + center * lax.rsqrt(spread_of(center) + width * 1e-5)
                total_ref[spot, :] = total
    for start in range(0, rows_total, 256):
        update(start, total_ref[pl.ds(start, 256), :])
    if not last:
        gather_ghosts(updated_ref, wanted_ref, send_refs)


def body(
    latents, mig_rows, mig_count, ghost_rows, ghost_count, neighbours, geometry, edge_w, node_w, geo_w, biases, gains
):
    owned = latents[0, 0]
    leave_rows, leave_count = mig_rows[0, 0], mig_count[0, 0]
    ghost_list, ghost_total = ghost_rows[0, 0], ghost_count[0, 0]
    tile_links = neighbours[0, 0]
    width = owned.shape[1]
    slots, tiles = tile_links.shape
    rows_total = geometry.shape[-1]
    ghosts = ghost_list.shape[1]
    table_rows = rows_total + 8 * ghosts
    all_links = links(lax.axis_size("gx"), lax.axis_size("gy"))
    sides = [link for link in all_links if None in link]
    groups = messages(all_links)
    rows_of = lambda count: jax.ShapeDtypeStruct((count, width), BF16)

    retained, *packets = pl.pallas_call(
        functools.partial(pack_kernel, sides),
        out_shape=[rows_of(owned.shape[0])] + [rows_of(leave_rows.shape[1])] * len(sides),
        in_specs=[HBM] * 3,
        out_specs=[VMEM] * (1 + len(sides)),
        scratch_shapes=[pltpu.VMEM((leave_rows.size, width), BF16)] + fetched(owned, leave_rows, leave_count, smem=(2,)),
        compiler_params=WHOLE,
        name="pack",
    )(owned, leave_rows, leave_count)
    arrivals = [swap(packet, link) for packet, link in zip(packets, sides)]

    feats = geometry.reshape(-1, rows_total)
    layers = edge_w.shape[0]
    deep = 2 * feats.shape[0] + width
    valid_ghosts = jnp.where(jnp.arange(ghosts)[None, :] < ghost_total[:, None], ghost_list, -1)
    wanted, kept = pl.pallas_call(
        functools.partial(want_kernel, sum(groups, [])),
        out_shape=[jax.ShapeDtypeStruct((len(all_links), ghosts, 128), F32), rows_of(owned.shape[0])],
        in_specs=[VMEM] * 2,
        out_specs=[VMEM] * 2,
        compiler_params=PARAMS,
        cost_estimate=pl.CostEstimate(flops=500_000_000, bytes_accessed=1_000_000, transcendentals=0),
        name="want",
    )(valid_ghosts, retained)

    extended, *sends = pl.pallas_call(
        functools.partial(build_kernel, sides),
        out_shape=[rows_of(rows_total)] + [rows_of(ghosts * len(group)) for group in groups],
        in_specs=[VMEM] * (2 + len(sides)),
        out_specs=[VMEM] * (1 + len(groups)),
        compiler_params=PARAMS,
        name="build",
    )(kept, *arrivals, wanted)

    turned, first_mats, second_mats = pl.pallas_call(
        static_kernel,
        out_shape=[
            jax.ShapeDtypeStruct((rows_total, 2 * feats.shape[0]), BF16),
            jax.ShapeDtypeStruct((layers, deep, slots * width), BF16),
            jax.ShapeDtypeStruct((layers, 2 * width, 2 * width), BF16),
        ],
        in_specs=[VMEM] * 3 + [pl.BlockSpec(memory_space=pl.ANY)],
        out_specs=[VMEM] * 3,
        compiler_params=PARAMS,
        cost_estimate=pl.CostEstimate(flops=1_000_000_000, bytes_accessed=3_000_000, transcendentals=0),
        name="static",
    )(feats, edge_w, geo_w, extended)

    for layer in range(layers):
        last = layer == layers - 1
        landed = exchange(sends, all_links, ghosts)
        base, own, empty = pl.pallas_call(
            functools.partial(receive_kernel, layer),
            out_shape=[
                jax.ShapeDtypeStruct((rows_total, slots * width), BF16),
                jax.ShapeDtypeStruct((rows_total, width), F32),
                jax.ShapeDtypeStruct((rows_total, width), F32),
            ],
            in_specs=[VMEM] * 6,
            out_specs=[VMEM] * 3,
            compiler_params=PARAMS,
            cost_estimate=pl.CostEstimate(flops=2_500_000_000, bytes_accessed=6_000_000, transcendentals=0),
            name="receive",
        )(extended, turned, first_mats, edge_w, biases, tile_links)
        outs = [rows_of(rows_total)] + ([] if last else [rows_of(ghosts * len(group)) for group in groups])
        extra = [] if last else [wanted]
        extended, *sends = pl.pallas_call(
            functools.partial(layer_kernel, layer, last, ghosts, all_links),
            out_shape=outs,
            in_specs=[VMEM] * 4 + [SMEM] + [VMEM] * (5 + len(all_links) + len(extra)),
            out_specs=[VMEM] * len(outs),
            scratch_shapes=[
                pltpu.VMEM((table_rows + 8, width), F32),
                pltpu.VMEM((rows_total, 2 * width), BF16),
                pltpu.VMEM((rows_total, width), F32),
            ],
            compiler_params=PARAMS,
            name="layer",
        )(extended, base, own, empty, tile_links, edge_w, node_w, second_mats, biases, gains, *landed, *extra)
    return extended[None, None]


def solution(mesh):
    block = lambda rank: P("gx", "gy", *[None] * rank)
    return jax.shard_map(
        body,
        mesh=mesh,
        in_specs=(block(2), block(2), block(1), block(2), block(1), block(2), block(3), P(), P(), P(), P(), P()),
        out_specs=block(2),
        check_vma=False,
    )
```
